256 devices in a mesh: tile: 64 (over y, x, z_lo, core), slab: 4 (over z_hi).
Axes of the slice: x: 4, y: 4, z: 8 (z_hi: 4, z_lo: 2; z = z_hi * 2 + z_lo), core: 2. Of those that a mesh axis runs over, the one named last changes fastest.
Arguments:
- counts: int32 [8192, 8, 512], P('tile', None, 'slab'), may hold values from 0 to 63
- fields: float32 [4, 8192, 8, 512], P(None, 'tile', None, 'slab'), may hold values from -20 to 20
- class_ids: int32 [8192, 8, 512], P('tile', None, 'slab'), may hold values from 0 to 7
- tf_table: float32 [8, 4, 6], replicated, may hold values from -2 to 2
Outputs:
- layers: float32 [4, 4, 8, 8192], P('slab', None, None, 'tile')
The draws below stay inside these ranges and needn't reach their ends.
All inputs are finite; a program needn't handle non-finite values.
Results may differ from the reference program's by a relative error of at most 0.0003.
Values sent between devices are 32-bit elements; how exact they have to be, the bound alone decides.
No kernel may reach another device: no remote copies, remote signals or barrier semaphores. Data moves between devices by JAX's collectives and lax.ppermute only.
A program may use at most 128 MiB of HBM per device.

```python
import math
import jax
import jax.numpy as jnp
from jax import lax

COLS = 128
ROWS = 8
DEPTH = 128
FIELDS = 4
CLASSES = 8
RADIUS = 4
NX = 8192
NZ = 512
N_TILE = 64
N_SLAB = 4


def table_shape(span):
    return ((NX + span - 1) // span, (ROWS + span - 1) // span, (NZ + span - 1) // span)


def spread_table(table, span):
    col_idx = jnp.arange(NX, dtype=jnp.int32) // span
    row_idx = jnp.arange(ROWS, dtype=jnp.int32) // span
    dep_idx = jnp.arange(NZ, dtype=jnp.int32) // span
    return table[..., col_idx[:, None, None], row_idx[None, :, None], dep_idx[None, None, :]]


def draw_counts(key, part):
    key = jax.random.fold_in(key, 11)
    key_wide, key_narrow, key_cells = jax.random.split(key, 3)
    wide = jax.random.randint(key_wide, table_shape(16), 0, 4, dtype=jnp.int32).at[0, 0, 0].set(3)
    narrow = jax.random.randint(key_narrow, table_shape(4), 0, 4, dtype=jnp.int32).at[0, 0, 0].set(3)
    expo = spread_table(wide, 16) + spread_table(narrow, 4)
    level = jnp.left_shift(jnp.ones_like(expo), expo)
    drawn = jax.random.randint(key_cells, (NX, ROWS, NZ), 0, level, dtype=jnp.int32)
    return drawn.at[0, 0, 0].set(level[0, 0, 0] - 1)


def draw_fields(key, part):
    key = jax.random.fold_in(key, 12)
    key_wide, key_narrow, key_cells = jax.random.split(key, 3)
    wide = jax.random.normal(key_wide, (FIELDS,) + table_shape(16), jnp.float32)
    narrow = jax.random.normal(key_narrow, (FIELDS,) + table_shape(4), jnp.float32)
    noise = jax.random.normal(key_cells, (FIELDS, NX, ROWS, NZ), jnp.float32)
    values = 3.0 * spread_table(wide, 16) + 2.0 * spread_table(narrow, 4) + 2.0 * noise
    return jnp.clip(values, -20.0, 20.0)


def place_ends(values, own_key, low, largest):
    place = [jax.random.randint(jax.random.fold_in(own_key, axis), (), 0, length) for axis, length in enumerate(values.shape)]
    widest = values.shape.index(max(values.shape))
    next_to = place[:widest] + [(place[widest] + 1) % values.shape[widest]] + place[widest + 1:]
    return values.at[tuple(place)].set(low).at[tuple(next_to)].set(largest)


def setup_inputs(seed: int = 0) -> dict:
    keys = jax.random.split(jax.random.key(seed), 5)
    return {
        "counts": draw_counts(jax.random.fold_in(keys[4], 71), 0),
        "fields": draw_fields(jax.random.fold_in(keys[4], 71), 0),
        "class_ids": place_ends(jax.random.randint(keys[2], (NX, ROWS, NZ), 0, CLASSES), jax.random.fold_in(keys[2], 1), 0, CLASSES - 1).astype(jnp.int32),
        "tf_table": jnp.clip(jax.random.uniform(keys[3], (CLASSES, 4, 6), jnp.float32, -2.0, 2.0), -2.0, 2.0),
    }


SPLAT = 2.0
OPTICAL = 0.5


def splat_taps():
    raw = [math.exp(-((offset - RADIUS) ** 2) / (2.0 * SPLAT * SPLAT)) for offset in range(2 * RADIUS + 1)]
    norm_total = sum(raw)
    return [value / norm_total for value in raw]


def blur_valid(volume, along):
    weights = splat_taps()
    length = volume.shape[along] - 2 * RADIUS
    running = weights[0] * lax.slice_in_dim(volume, 0, length, axis=along)
    for offset in range(1, 2 * RADIUS + 1):
        running = running + weights[offset] * lax.slice_in_dim(volume, offset, offset + length, axis=along)
    return running


def blur_padded(volume, along):
    widths = [(0, 0)] * volume.ndim
    widths[along] = (RADIUS, RADIUS)
    return blur_valid(jnp.pad(volume, widths), along)


def combine_pair(nearer, farther):
    return (nearer[0] + nearer[1][None] * farther[0], nearer[1] * farther[1])


def reference(counts, fields, class_ids, tf_table):
    def render_block(block_index):
        start = block_index * COLS - RADIUS
        positions = start + jnp.arange(COLS + 2 * RADIUS, dtype=jnp.int32)
        inside = ((positions >= 0) & (positions < NX)).astype(jnp.float32)
        safe_pos = jnp.clip(positions, 0, NX - 1).astype(jnp.int32)
        density = jnp.log1p(jnp.take(counts, safe_pos, axis=0).astype(jnp.float32))
        others = jnp.take(fields, safe_pos, axis=1)
        volume = jnp.concatenate([density[None], others], 0) * inside[None, :, None, None]
        volume = blur_padded(volume, 2)
        volume = blur_valid(volume, 1)
        smooth = blur_padded(volume, 3)
        block_cls = lax.dynamic_slice_in_dim(class_ids, (block_index * COLS).astype(jnp.int32), COLS, 0)
        coefficients = tf_table.reshape(CLASSES, 24)[block_cls]
        linears = []
        for channel in range(4):
            linear = coefficients[..., channel * 6] * smooth[0]
            for field_index in range(1, 5):
                linear = linear + coefficients[..., channel * 6 + field_index] * smooth[field_index]
            linears.append(linear + coefficients[..., channel * 6 + 5])
        emitted = jax.nn.sigmoid(jnp.stack(linears[:3], 0))
        depth_step = jax.nn.softplus(linears[3]) * (OPTICAL / NZ)
        opacity = -jnp.expm1(-depth_step)
        step_slabs = depth_step.reshape(COLS, ROWS, N_SLAB, DEPTH)
        cumulative = jnp.cumsum(step_slabs, axis=-1)
        before = jnp.concatenate([jnp.zeros_like(cumulative[..., :1]), cumulative[..., :-1]], -1)
        shading = opacity.reshape(COLS, ROWS, N_SLAB, DEPTH) * jnp.exp(-before)
        radiance = jnp.sum(emitted.reshape(3, COLS, ROWS, N_SLAB, DEPTH) * shading[None], axis=-1)
        transmit = jnp.exp(-jnp.sum(step_slabs, axis=-1))
        front_pair = (jnp.zeros((3, COLS, ROWS), jnp.float32), jnp.ones((COLS, ROWS), jnp.float32))
        outputs = []
        for slab_index in range(N_SLAB):
            own_pair = (radiance[..., slab_index], transmit[..., slab_index])
            shown = front_pair[0] + front_pair[1][None] * own_pair[0]
            alpha_out = 1.0 - front_pair[1] * own_pair[1]
            outputs.append(jnp.concatenate([shown, alpha_out[None]], 0))
            front_pair = combine_pair(front_pair, own_pair)
        return jnp.transpose(jnp.stack(outputs, 0), (0, 1, 3, 2))

    blocks = lax.map(render_block, jnp.arange(N_TILE, dtype=jnp.int32))
    return jnp.transpose(blocks, (1, 2, 3, 0, 4)).reshape(N_SLAB, 4, ROWS, NX)
```

```python
import functools
import math

import jax
import jax.numpy as jnp
import numpy as np
from jax import lax
from jax.experimental import pallas as pl
from jax.experimental.pallas import tpu as pltpu
from jax.sharding import PartitionSpec as P

CLASSES = 8
RADIUS = 4
SPLAT = 2.0
OPTICAL = 0.5
COLS, ROWS, DEPTH = 128, 8, 128
F32, BF16 = jnp.float32, jnp.bfloat16
VMEM = pltpu.VMEM


def splat_taps():
    raw = [
        math.exp(-((offset - RADIUS) ** 2) / (2.0 * SPLAT * SPLAT))
        for offset in range(2 * RADIUS + 1)
    ]
    norm_total = sum(raw)
    return [value / norm_total for value in raw]


W = splat_taps()


def tap(offset):
    return W[offset + RADIUS] if abs(offset) <= RADIUS else 0.0


def depth_matrix():
    full = np.zeros((DEPTH + 8, DEPTH), np.float64)
    targets = list(range(DEPTH)) + [-4, -3, -2, -1] + [DEPTH + i for i in range(4)]
    for row, target in enumerate(targets):
        for cell in range(DEPTH):
            full[row, cell] = tap(cell - target)
    high = full.astype(jnp.bfloat16)
    low = (full - high.astype(np.float64)).astype(jnp.bfloat16)
    top = np.concatenate([high, high], 1)
    bottom = np.concatenate([low, np.zeros_like(low)], 1)
    return np.concatenate([top, bottom], 0)


def symmetric(values):
    total = values[4] * W[4]
    for reach in range(1, RADIUS + 1):
        total = total + (values[4 - reach] + values[4 + reach]) * W[4 + reach]
    return total


def blur_rows(rows):
    out = []
    for target in range(ROWS):
        total = rows[target] * W[4]
        for reach in range(1, RADIUS + 1):
            low, high = target - reach, target + reach
            if low >= 0 and high < ROWS:
                total = total + (rows[low] + rows[high]) * W[4 + reach]
            elif low >= 0:
                total = total + rows[low] * W[4 + reach]
            elif high < ROWS:
                total = total + rows[high] * W[4 + reach]
        out.append(total)
    return out


def columns_kernel(table, counts, fields, classes, blurred, class_t, tables, density, mix):
    lane = lax.broadcasted_iota(jnp.int32, (ROWS, 128), 1)
    for channel in range(4):
        for coefficient in range(6):
            scale = 0.5 if channel < 3 else 1.0
            entry = jnp.zeros((ROWS, 128), F32)
            for label in range(CLASSES):
                entry = jnp.where(lane == label, table[label, channel, coefficient] * scale, entry)
            tables[channel * 6 + coefficient] = entry

    density[...] = jnp.log1p(counts[...].astype(F32))

    def block(source, field, first, lo, hi):
        def column(offset):
            if not lo <= offset < hi:
                return None
            return source(first + offset)

        near = {offset: column(offset) for offset in range(-4, 12)}
        for target in range(8):
            total = near[target] * W[4]
            for reach in range(1, RADIUS + 1):
                low, high = near[target - reach], near[target + reach]
                if low is not None and high is not None:
                    total = total + (low + high) * W[4 + reach]
                elif low is not None:
                    total = total + low * W[4 + reach]
                elif high is not None:
                    total = total + high * W[4 + reach]
            mix[pl.ds(target * 8, 8), :] = total
        rows = blur_rows([mix[pl.ds(row, 8, stride=8), :] for row in range(ROWS)])
        for row in range(ROWS):
            blurred[field, row, pl.ds(first, 8), :] = rows[row]

    def sweep(source, field):
        block(source, field, 0, 0, 12)

        def body(index, carry):
            block(source, field, pl.multiple_of(index * 8, 8), -4, 12)
            return carry

        lax.fori_loop(1, COLS // 8 - 1, body, 0)
        block(source, field, COLS - 8, -4, 8)

    sweep(lambda column: density[column], 0)

    def over_fields(field, carry):
        sweep(lambda column: fields[field, column], field + 1)
        return carry

    lax.fori_loop(0, 4, over_fields, 0)

    flat = classes.reshape(COLS * ROWS, DEPTH)
    flat_t = class_t.reshape(DEPTH * ROWS, COLS)
    for row in range(ROWS):
        plane = flat[pl.ds(row, COLS, stride=ROWS), :]
        flat_t[pl.ds(row, DEPTH, stride=ROWS), :] = plane.T


def depth_kernel(n_tile, blurred, left, right, matrix, smooth, outward, edge, mix):
    tile = lax.axis_index("tile")
    has_left = (tile > 0).astype(F32)
    has_right = (tile < n_tile - 1).astype(F32)
    for field in range(5):
        for j in range(4):
            total = left[field, j] * tap(-4)
            for h in range(j + 1, 4):
                total = total + left[field, h] * tap(h - 4 - j)
            mix[pl.ds(j * 8, 8), :] = total * has_left
            total = right[field, j] * tap(4)
            for h in range(j):
                total = total + right[field, h] * tap(4 + h - j)
            mix[pl.ds(32 + j * 8, 8), :] = total * has_right
        rows = blur_rows([mix[pl.ds(row, 8, stride=8), :] for row in range(ROWS)])
        for row in range(ROWS):
            edge[field, row] = rows[row]

    sub = lax.broadcasted_iota(jnp.int32, (8, 128), 0)
    is_left = sub < 4
    flat = smooth.reshape(5, DEPTH * ROWS, COLS)
    flat_out = outward.reshape(5, 8 * ROWS, COLS)

    def body(index, carry):
        field = index // 4
        pair = index % 4
        parts = []
        for j in range(2):
            row = pair * 2 + j
            extra = edge[field, row]
            plane = blurred[field, row]
            parts.append(plane[:8] + jnp.where(is_left, extra, 0.0))
            parts.append(plane[8:120])
            parts.append(plane[120:] + jnp.where(is_left, 0.0, extra))
        both = jnp.concatenate(parts, 0)
        high = both.astype(BF16)
        low = (both - high.astype(F32)).astype(BF16)
        stack = jnp.concatenate([high, low], 1)
        out = lax.dot_general(
            matrix[...], stack, (((1,), (1,)), ((), ())), preferred_element_type=F32
        )
        out = out[: DEPTH + 8] + out[DEPTH + 8 :]
        for j in range(2):
            row = pair * 2 + j
            half = out[:, j * 128 : (j + 1) * 128]
            flat[field, pl.ds(row, DEPTH, stride=ROWS), :] = half[:DEPTH]
            flat_out[field, pl.ds(row, 8, stride=ROWS), :] = half[DEPTH:]
        return carry

    lax.fori_loop(0, 20, body, 0)


def shade_cell(values, label, tables, scale, state):
    trans, s_sum, r_sum, g_sum, b_sum, step_sum = state
    linears = []
    for channel in range(4):
        entry = [
            jnp.take_along_axis(
                tables[channel * 6 + i], label, axis=1, mode="promise_in_bounds"
            )
            for i in range(6)
        ]
        linear = entry[0] * values[0] + entry[5]
        for i in range(1, 5):
            linear = linear + entry[i] * values[i]
        linears.append(linear)
    tints = [jnp.tanh(linear) for linear in linears[:3]]
    x = linears[3]
    t = jnp.exp(-jnp.abs(x))
    series = t * (1.0 - t * (1.0 / 2 - t * (1.0 / 3 - t * (1.0 / 4))))
    soft = jnp.maximum(x, 0.0) + jnp.where(t < 0.01, series, jnp.log(1.0 + t))
    step = soft * scale
    opacity = step * (
        1.0 - step * (1.0 / 2 - step * (1.0 / 6 - step * (1.0 / 24 - step * (1.0 / 120))))
    )
    shade = trans * opacity
    return (
        trans - shade,
        s_sum + shade,
        r_sum + shade * tints[0],
        g_sum + shade * tints[1],
        b_sum + shade * tints[2],
        step_sum + step,
    )


def fresh_state():
    zero = jnp.zeros((ROWS, COLS), F32)
    return (jnp.ones((ROWS, COLS), F32), zero, zero, zero, zero, zero)


def inner_kernel(scale, smooth, class_t, tables, out):
    unroll = 8

    def body(index, state):
        start = 4 + index * unroll
        for k in range(unroll):
            depth = start + k
            state = shade_cell(
                [smooth[f, depth] for f in range(5)], class_t[depth], tables, scale, state
            )
        return state

    state = lax.fori_loop(0, (DEPTH - 8) // unroll, body, fresh_state())
    for i in range(6):
        out[i] = state[i]


def edge_kernel(scale, n_slab, smooth, class_t, tables, inner, front, behind, out):
    slab = lax.axis_index("slab")
    has_front = (slab > 0).astype(F32)
    has_behind = (slab < n_slab - 1).astype(F32)
    state = fresh_state()
    for k in range(4):
        values = [smooth[f, k] + front[f, k] * has_front for f in range(5)]
        state = shade_cell(values, class_t[k], tables, scale, state)
    trans = state[0]
    state = (
        trans * inner[0],
        state[1] + trans * inner[1],
        state[2] + trans * inner[2],
        state[3] + trans * inner[3],
        state[4] + trans * inner[4],
        state[5] + inner[5],
    )
    for k in range(4):
        depth = DEPTH - 4 + k
        values = [smooth[f, depth] + behind[f, k] * has_behind for f in range(5)]
        state = shade_cell(values, class_t[depth], tables, scale, state)
    for i in range(3):
        out[i] = 0.5 * (state[1] + state[2 + i])
    out[3] = jnp.exp(-state[5])


def in_vmem(*arrays):
    return tuple(pltpu.with_memory_space_constraint(a, VMEM) for a in arrays)


SPEC = pl.BlockSpec(memory_space=VMEM)
SMEM_SPEC = pl.BlockSpec(memory_space=pltpu.SMEM)
PARAMS = pltpu.CompilerParams(vmem_limit_bytes=32 * 1024 * 1024)


def ring(value, axis, shift):
    count = lax.axis_size(axis)
    return lax.ppermute(value, axis, [(i, (i + shift) % count) for i in range(count)])


def on_device(counts, fields, class_ids, tf_table):
    n_tile, n_slab = lax.axis_size("tile"), lax.axis_size("slab")
    scale = OPTICAL / (DEPTH * n_slab)

    def side(start):
        dens = jnp.log1p(counts[start : start + RADIUS].astype(F32))
        return jnp.concatenate([dens[None], fields[:, start : start + RADIUS]], 0)

    from_left = ring(side(COLS - RADIUS), "tile", 1)
    from_right = ring(side(0), "tile", -1)

    blurred, class_t, tables = pl.pallas_call(
        columns_kernel,
        out_shape=[
            VMEM((5, ROWS, COLS, DEPTH), F32),
            VMEM((DEPTH, ROWS, COLS), jnp.int32),
            VMEM((24, ROWS, 128), F32),
        ],
        in_specs=[SMEM_SPEC, SPEC, SPEC, SPEC],
        out_specs=[SPEC] * 3,
        scratch_shapes=[VMEM((COLS, ROWS, DEPTH), F32), VMEM((64, 128), F32)],
        compiler_params=PARAMS,
        name="columns",
    )(tf_table, *in_vmem(counts, fields, class_ids))

    smooth, outward = pl.pallas_call(
        functools.partial(depth_kernel, n_tile),
        out_shape=[VMEM((5, DEPTH, ROWS, COLS), F32), VMEM((5, 8, ROWS, COLS), F32)],
        in_specs=[SPEC] * 4,
        out_specs=[SPEC] * 2,
        scratch_shapes=[VMEM((5, ROWS, 8, DEPTH), F32), VMEM((64, 128), F32)],
        compiler_params=PARAMS,
        name="depth",
    )(*in_vmem(blurred, from_left, from_right, jnp.asarray(depth_matrix())))

    from_behind = ring(outward[:, :4], "slab", -1)
    from_front = ring(outward[:, 4:], "slab", 1)

    inner = pl.pallas_call(
        functools.partial(inner_kernel, scale),
        out_shape=VMEM((6, ROWS, COLS), F32),
        in_specs=[SPEC] * 3,
        out_specs=SPEC,
        compiler_params=PARAMS,
        name="inner",
    )(*in_vmem(smooth, class_t, tables))

    pair = pl.pallas_call(
        functools.partial(edge_kernel, scale, n_slab),
        out_shape=VMEM((4, ROWS, COLS), F32),
        in_specs=[SPEC] * 6,
        out_specs=SPEC,
        compiler_params=PARAMS,
        name="edges",
    )(*in_vmem(smooth, class_t, tables, inner, from_front, from_behind))

    slab = lax.axis_index("slab")
    others = {shift: ring(pair, "slab", shift) for shift in range(1, n_slab)}
    front_rad = jnp.zeros((3, ROWS, COLS), F32)
    front_tra = jnp.ones((ROWS, COLS), F32)
    for shift in range(n_slab - 1, 0, -1):
        there = slab >= shift
        front_rad = front_rad + front_tra * jnp.where(there, others[shift][:3], 0.0)
        front_tra = front_tra * jnp.where(there, others[shift][3], 1.0)
    shown = front_rad + front_tra * pair[:3]
    alpha = 1.0 - front_tra * pair[3]
    return jnp.concatenate([shown, alpha[None]], 0)[None]


def solution(mesh):
    return jax.shard_map(
        on_device,
        mesh=mesh,
        in_specs=(
            P("tile", None, "slab"),
            P(None, "tile", None, "slab"),
            P("tile", None, "slab"),
            P(),
        ),
        out_specs=P("slab", None, None, "tile"),
        check_vma=False,
    )
```

```python
import functools
import math

import jax
import jax.numpy as jnp
import numpy as np
from jax import lax
from jax.experimental import pallas as pl
from jax.experimental.pallas import tpu as pltpu
from jax.sharding import PartitionSpec as P

CLASSES = 8
RADIUS = 4
SPLAT = 2.0
OPTICAL = 0.5
COLS, ROWS, DEPTH = 128, 8, 128
F32, BF16 = jnp.float32, jnp.bfloat16
VMEM = pltpu.VMEM


def splat_taps():
    raw = [
        math.exp(-((offset - RADIUS) ** 2) / (2.0 * SPLAT * SPLAT))
        for offset in range(2 * RADIUS + 1)
    ]
    norm_total = sum(raw)
    return [value / norm_total for value in raw]


W = splat_taps()


def tap(offset):
    return W[offset + RADIUS] if abs(offset) <= RADIUS else 0.0


def split_const(full):
    high = full.astype(jnp.bfloat16)
    return high, (full - high.astype(np.float64)).astype(jnp.bfloat16)


def depth_matrix():
    full = np.zeros((DEPTH + 8, DEPTH), np.float64)
    targets = list(range(DEPTH)) + [-4, -3, -2, -1] + [DEPTH + i for i in range(4)]
    for row, target in enumerate(targets):
        for cell in range(DEPTH):
            full[row, cell] = tap(cell - target)
    high, low = split_const(full)
    top = np.concatenate([high, high], 1)
    bottom = np.concatenate([low, np.zeros_like(low)], 1)
    return np.concatenate([top, bottom], 0)


def plane_matrix(targets, cells):
    full = np.zeros((ROWS, len(targets), len(cells), ROWS), np.float64)
    for to_row in range(ROWS):
        for i, target in enumerate(targets):
            for j, cell in enumerate(cells):
                for row in range(ROWS):
                    full[to_row, i, j, row] = tap(cell - target) * tap(row - to_row)
    return np.concatenate(split_const(full.reshape(ROWS * len(targets), len(cells) * ROWS)), 0)


WIDE = 24
INNER = COLS - 2 * RADIUS
RIM = list(range(-RADIUS, 8)) + list(range(COLS - 8, COLS + RADIUS))
RIM_TARGETS = list(range(COLS - RADIUS, COLS)) + list(range(RADIUS))


def split(value):
    high = value.astype(BF16)
    return high, (value - high.astype(F32)).astype(BF16)


def plane_blur(matrix, cells):
    rows = matrix.shape[0] // 2
    out = jnp.dot(
        matrix[...], jnp.concatenate(split(cells), 1), preferred_element_type=F32
    )
    return out[:rows, :DEPTH] + out[:rows, DEPTH:] + out[rows:, :DEPTH]


def pack_kernel(counts, fields, first, last, count_rows, sems):
    copies = []
    for i, (ref, start) in enumerate(((first, 0), (last, COLS - RADIUS))):
        copies.append(
            pltpu.make_async_copy(
                counts.at[pl.ds(start, RADIUS)], count_rows.at[i], sems.at[2 * i]
            )
        )
        copies.append(
            pltpu.make_async_copy(
                fields.at[:, pl.ds(start, RADIUS)], ref.at[pl.ds(1, 4)], sems.at[2 * i + 1]
            )
        )
    for copy in copies:
        copy.start()
    for copy in copies:
        copy.wait()
    first[0] = jnp.log(1.0 + count_rows[0].astype(F32))
    last[0] = jnp.log(1.0 + count_rows[1].astype(F32))


def columns_kernel(
    table, matrix, counts, fields, classes,
    blurred, rim, class_t, tables,
    count_v, field_v, class_v, density, sems,
):
    copies = [pltpu.make_async_copy(counts, count_v, sems.at[0])]
    for field in range(4):
        copies.append(
            pltpu.make_async_copy(fields.at[field], field_v.at[field], sems.at[field + 1])
        )
    copies.append(pltpu.make_async_copy(classes, class_v, sems.at[5]))
    for copy in copies:
        copy.start()

    lane = lax.broadcasted_iota(jnp.int32, (CLASSES, CLASSES), 1)
    row_index = lax.broadcasted_iota(jnp.int32, (CLASSES, CLASSES), 0)
    for channel in range(4):
        scale = 0.5 if channel < 3 else 1.0
        for coefficient in range(6):
            per_class = jnp.broadcast_to(
                table[coefficient, channel : channel + 1, :], (CLASSES, CLASSES)
            )
            column = jnp.sum(
                jnp.where(lane == row_index, per_class, 0.0), axis=1, keepdims=True
            )
            tables[channel * 6 + coefficient] = jnp.broadcast_to(column * scale, (CLASSES, 128))

    def sweep(source, field):
        rim[field, pl.ds(0, 64), :] = source[pl.ds(0, 64), :]
        rim[field, pl.ds(64, 64), :] = source[pl.ds((COLS - 8) * ROWS, 64), :]

        for step in range(INNER // WIDE):
            out = plane_blur(matrix, source[pl.ds(step * WIDE * ROWS, (WIDE + 8) * ROWS), :])
            for row in range(ROWS):
                blurred[field, row, pl.ds(step * WIDE, WIDE), :] = out[
                    row * WIDE : (row + 1) * WIDE
                ]

    copies[0].wait()
    density[...] = jnp.log(1.0 + count_v[...].astype(F32))
    sweep(density.reshape(COLS * ROWS, DEPTH), 0)

    for field in range(4):
        copies[field + 1].wait()
        sweep(field_v.at[field].reshape(COLS * ROWS, DEPTH), field + 1)

    copies[5].wait()
    flat = class_v.reshape(COLS * ROWS, DEPTH)
    flat_t = class_t.reshape(DEPTH * ROWS, COLS)
    for row in range(ROWS):
        plane = flat[pl.ds(row, COLS, stride=ROWS), :]
        flat_t[pl.ds(row, DEPTH, stride=ROWS), :] = pltpu.roll(plane.T, COLS - RADIUS, 1)


def depth_kernel(n_tile, blurred, rim, left, right, rim_matrix, matrix, smooth, outward, edge):
    tile = lax.axis_index("tile")
    has_left = (tile > 0).astype(F32)
    has_right = (tile < n_tile - 1).astype(F32)
    side = RADIUS * ROWS
    for field in range(5):
        cells = jnp.concatenate(
            [
                left[field].reshape(side, DEPTH) * has_left,
                rim[field],
                right[field].reshape(side, DEPTH) * has_right,
            ],
            0,
        )
        edge[field] = plane_blur(rim_matrix, cells).reshape(ROWS, 8, DEPTH)

    flat = smooth.reshape(5, DEPTH * ROWS, COLS)
    flat_out = outward.reshape(5, 8 * ROWS, COLS)

    def body(index, carry):
        field = index // 4
        pair = index % 4
        parts = []
        for j in range(2):
            parts += [blurred[field, pair * 2 + j], edge[field, pair * 2 + j]]
        stack = jnp.concatenate(split(jnp.concatenate(parts, 0)), 1)
        out = lax.dot_general(
            matrix[...], stack, (((1,), (1,)), ((), ())), preferred_element_type=F32
        )
        out = out[: DEPTH + 8] + out[DEPTH + 8 :]
        for j in range(2):
            row = pair * 2 + j
            half = out[:, j * 128 : (j + 1) * 128]
            flat[field, pl.ds(row, DEPTH, stride=ROWS), :] = half[:DEPTH]
            flat_out[field, pl.ds(row, 8, stride=ROWS), :] = half[DEPTH:]
        return carry

    lax.fori_loop(0, 20, body, 0, unroll=10)


def shade_cell(values, label, tables, scale, state):
    trans, s_sum, r_sum, g_sum, b_sum, step_sum = state
    linears = []
    for channel in range(4):
        entry = [
            jnp.take_along_axis(
                tables[channel * 6 + i], label, axis=0, mode="promise_in_bounds"
            )
            for i in range(6)
        ]
        linear = entry[0] * values[0] + entry[5]
        for i in range(1, 5):
            linear = linear + entry[i] * values[i]
        linears.append(linear)
    tints = [jnp.tanh(linear) for linear in linears[:3]]
    x = linears[3]
    t = jnp.exp(-jnp.abs(x))
    series = t * (1.0 - t * (1.0 / 2 - t * (1.0 / 3 - t * (1.0 / 4))))
    soft = jnp.maximum(x, 0.0) + jnp.where(t < 0.01, series, jnp.log(1.0 + t))
    step = soft * scale
    opacity = step * (
        1.0 - step * (1.0 / 2 - step * (1.0 / 6 - step * (1.0 / 24 - step * (1.0 / 120))))
    )
    shade = trans * opacity
    return (
        trans - shade,
        s_sum + shade,
        r_sum + shade * tints[0],
        g_sum + shade * tints[1],
        b_sum + shade * tints[2],
        step_sum + step,
    )


def fresh_state():
    zero = jnp.zeros((ROWS, COLS), F32)
    return (jnp.ones((ROWS, COLS), F32), zero, zero, zero, zero, zero)


def inner_kernel(scale, smooth, class_t, tables, out):
    unroll = 8

    def body(index, state):
        start = 4 + index * unroll
        for k in range(unroll):
            depth = start + k
            state = shade_cell(
                [smooth[f, depth] for f in range(5)], class_t[depth], tables, scale, state
            )
        return state

    state = lax.fori_loop(0, (DEPTH - 8) // unroll, body, fresh_state())
    for i in range(6):
        out[i] = state[i]


def edge_kernel(scale, n_slab, smooth, class_t, tables, inner, front, behind, out):
    slab = lax.axis_index("slab")
    has_front = (slab > 0).astype(F32)
    has_behind = (slab < n_slab - 1).astype(F32)
    state = fresh_state()
    for k in range(4):
        values = [smooth[f, k] + front[f, k] * has_front for f in range(5)]
        state = shade_cell(values, class_t[k], tables, scale, state)
    trans = state[0]
    state = (
        trans * inner[0],
        state[1] + trans * inner[1],
        state[2] + trans * inner[2],
        state[3] + trans * inner[3],
        state[4] + trans * inner[4],
        state[5] + inner[5],
    )
    for k in range(4):
        depth = DEPTH - 4 + k
        values = [smooth[f, depth] + behind[f, k] * has_behind for f in range(5)]
        state = shade_cell(values, class_t[depth], tables, scale, state)
    for i in range(3):
        out[i] = pltpu.roll(0.5 * (state[1] + state[2 + i]), RADIUS, 1)
    out[3] = pltpu.roll(jnp.exp(-state[5]), RADIUS, 1)


def in_vmem(*arrays):
    return tuple(pltpu.with_memory_space_constraint(a, VMEM) for a in arrays)


def in_hbm(*arrays):
    return tuple(pltpu.with_memory_space_constraint(a, pltpu.HBM) for a in arrays)


SPEC = pl.BlockSpec(memory_space=VMEM)
HBM_SPEC = pl.BlockSpec(memory_space=pltpu.HBM)
PARAMS = pltpu.CompilerParams(vmem_limit_bytes=32 * 1024 * 1024)


def ring(value, axis, shift):
    count = lax.axis_size(axis)
    return lax.ppermute(value, axis, [(i, (i + shift) % count) for i in range(count)])


def on_device(counts, fields, class_ids, tf_table):
    n_tile, n_slab = lax.axis_size("tile"), lax.axis_size("slab")
    scale = OPTICAL / (DEPTH * n_slab)

    first, last = pl.pallas_call(
        pack_kernel,
        out_shape=[VMEM((5, RADIUS, ROWS, DEPTH), F32)] * 2,
        in_specs=[HBM_SPEC] * 2,
        out_specs=[SPEC] * 2,
        scratch_shapes=[VMEM((2, RADIUS, ROWS, DEPTH), jnp.int32), pltpu.SemaphoreType.DMA((4,))],
        compiler_params=PARAMS,
        name="pack",
    )(*in_hbm(counts, fields))

    from_left = ring(last, "tile", 1)
    from_right = ring(first, "tile", -1)

    step_matrix = plane_matrix(list(range(RADIUS, RADIUS + WIDE)), list(range(WIDE + 8)))
    blurred, rim, class_t, tables = pl.pallas_call(
        columns_kernel,
        out_shape=[
            VMEM((5, ROWS, INNER, DEPTH), F32),
            VMEM((5, 16 * ROWS, DEPTH), F32),
            VMEM((DEPTH, ROWS, COLS), jnp.int32),
            VMEM((24, ROWS, 128), F32),
        ],
        in_specs=[SPEC] * 2 + [HBM_SPEC] * 3,
        out_specs=[SPEC] * 4,
        scratch_shapes=[
            VMEM((COLS, ROWS, DEPTH), jnp.int32),
            VMEM((4, COLS, ROWS, DEPTH), F32),
            VMEM((COLS, ROWS, DEPTH), jnp.int32),
            VMEM((COLS, ROWS, DEPTH), F32),
            pltpu.SemaphoreType.DMA((6,)),
        ],
        compiler_params=PARAMS,
        name="columns",
    )(*in_vmem(jnp.transpose(tf_table, (2, 1, 0)), jnp.asarray(step_matrix)), *in_hbm(counts, fields, class_ids))

    rim_matrix = plane_matrix(RIM_TARGETS, RIM)
    smooth, outward = pl.pallas_call(
        functools.partial(depth_kernel, n_tile),
        out_shape=[VMEM((5, DEPTH, ROWS, COLS), F32), VMEM((5, 8, ROWS, COLS), F32)],
        in_specs=[SPEC] * 6,
        out_specs=[SPEC] * 2,
        scratch_shapes=[VMEM((5, ROWS, 8, DEPTH), F32)],
        compiler_params=PARAMS,
        name="depth",
    )(
        *in_vmem(
            blurred, rim, from_left, from_right,
            jnp.asarray(rim_matrix), jnp.asarray(depth_matrix()),
        )
    )

    from_behind = ring(outward[:, :4], "slab", -1)
    from_front = ring(outward[:, 4:], "slab", 1)

    inner = pl.pallas_call(
        functools.partial(inner_kernel, scale),
        out_shape=VMEM((6, ROWS, COLS), F32),
        in_specs=[SPEC] * 3,
        out_specs=SPEC,
        compiler_params=PARAMS,
        name="inner",
    )(*in_vmem(smooth, class_t, tables))

    pair = pl.pallas_call(
        functools.partial(edge_kernel, scale, n_slab),
        out_shape=VMEM((4, ROWS, COLS), F32),
        in_specs=[SPEC] * 6,
        out_specs=SPEC,
        compiler_params=PARAMS,
        name="edges",
    )(*in_vmem(smooth, class_t, tables, inner, from_front, from_behind))

    slab = lax.axis_index("slab")
    others = {shift: ring(pair, "slab", shift) for shift in (2, 1, 3)}
    front_rad = jnp.zeros((3, ROWS, COLS), F32)
    front_tra = jnp.ones((ROWS, COLS), F32)
    for shift in (3, 2, 1):
        there = slab >= shift
        front_rad = front_rad + front_tra * jnp.where(there, others[shift][:3], 0.0)
        front_tra = front_tra * jnp.where(there, others[shift][3], 1.0)
    shown = front_rad + front_tra * pair[:3]
    alpha = 1.0 - front_tra * pair[3]
    return jnp.concatenate([shown, alpha[None]], 0)[None]


def solution(mesh):
    return jax.shard_map(
        on_device,
        mesh=mesh,
        in_specs=(
            P("tile", None, "slab"),
            P(None, "tile", None, "slab"),
            P("tile", None, "slab"),
            P(),
        ),
        out_specs=P("slab", None, None, "tile"),
        check_vma=False,
    )
```

```python
import functools
import math

import jax
import jax.numpy as jnp
import numpy as np
from jax import lax
from jax.experimental import pallas as pl
from jax.experimental.pallas import tpu as pltpu
from jax.sharding import PartitionSpec as P

CLASSES = 8
RADIUS = 4
SPLAT = 2.0
OPTICAL = 0.5
COLS, ROWS, DEPTH = 128, 8, 128
F32, BF16 = jnp.float32, jnp.bfloat16
VMEM = pltpu.VMEM


def splat_taps():
    raw = [
        math.exp(-((offset - RADIUS) ** 2) / (2.0 * SPLAT * SPLAT))
        for offset in range(2 * RADIUS + 1)
    ]
    norm_total = sum(raw)
    return [value / norm_total for value in raw]


W = splat_taps()


def tap(offset):
    return W[offset + RADIUS] if abs(offset) <= RADIUS else 0.0


def split_const(full):
    high = full.astype(jnp.bfloat16)
    return high, (full - high.astype(np.float64)).astype(jnp.bfloat16)


def split_rows(full):
    high, low = split_const(full)
    top = np.concatenate([high, high], 1)
    bottom = np.concatenate([low, np.zeros_like(low)], 1)
    return np.concatenate([top, bottom], 0)


def depth_matrix(targets):
    return split_rows(
        np.array([[tap(cell - target) for cell in range(DEPTH)] for target in targets])
    )


def plane_matrix(targets, cells):
    full = np.zeros((ROWS, len(targets), len(cells), ROWS), np.float64)
    for to_row in range(ROWS):
        for i, target in enumerate(targets):
            for j, cell in enumerate(cells):
                for row in range(ROWS):
                    full[to_row, i, j, row] = tap(cell - target) * tap(row - to_row)
    return split_rows(full.reshape(ROWS * len(targets), len(cells) * ROWS))


WIDE = 8
INNER = COLS - 2 * RADIUS
FRONT_TARGETS = list(range(-RADIUS, RADIUS))
INNER_TARGETS = list(range(RADIUS, DEPTH - RADIUS))
BACK_TARGETS = list(range(DEPTH - RADIUS, DEPTH + RADIUS))
BODY = 112


def split(value):
    high = value.astype(BF16)
    return high, (value - high.astype(F32)).astype(BF16)


def plane_blur(matrix, stack):
    out = jnp.dot(matrix[...], stack, preferred_element_type=F32)
    rows = matrix.shape[0] // 2
    return out[:rows] + out[rows:]


def pack_kernel(counts, fields, far, near, count_rows, sems):
    even = lax.axis_index("tile") % 2 == 0
    copies = []
    for i, (ref, at_start) in enumerate(((far, even), (near, jnp.logical_not(even)))):
        cells = pl.ds(jnp.where(at_start, 0, COLS - RADIUS), RADIUS)
        copies.append(pltpu.make_async_copy(counts.at[cells], count_rows.at[i], sems.at[2 * i]))
        copies.append(
            pltpu.make_async_copy(fields.at[:, cells], ref.at[pl.ds(1, 4)], sems.at[2 * i + 1])
        )
    for copy in copies:
        copy.start()
    for copy in copies:
        copy.wait()
    far[0] = jnp.log(1.0 + count_rows[0].astype(F32))
    near[0] = jnp.log(1.0 + count_rows[1].astype(F32))


def columns_kernel(
    matrix, end_matrix, counts, fields, classes,
    bodies, last, rim, class_v, send,
    count_v, field_v, high, low, sems,
):
    copies = [pltpu.make_async_copy(counts, count_v, sems.at[0])]
    for field in range(4):
        copies.append(
            pltpu.make_async_copy(fields.at[field], field_v.at[field], sems.at[field + 1])
        )
    copies.append(pltpu.make_async_copy(classes, class_v, sems.at[5]))
    for copy in copies:
        copy.start()

    def prepare(source, field):
        rim[field, pl.ds(0, 64), :] = source[pl.ds(0, 64), :]
        rim[field, pl.ds(64, 64), :] = source[pl.ds((COLS - 8) * ROWS, 64), :]
        high[field], low[field] = split(source[...])

    def product(windows):
        sides = []
        for field, step in windows:
            cells = pl.ds(step * WIDE * ROWS, 2 * WIDE * ROWS)
            sides.append(jnp.concatenate([high[field, cells, :], low[field, cells, :]], 0))
        return plane_blur(matrix, jnp.concatenate(sides, 1))

    def sweep(field):
        for step in range(0, BODY // WIDE, 2):
            out = product([(field, step), (field, step + 1)])
            for row in range(ROWS):
                cut = out[row * WIDE : (row + 1) * WIDE]
                tile = jnp.concatenate([cut[:, :DEPTH], cut[:, DEPTH:]], 0)
                bodies[field * 4 + row // 2, row % 2, pl.ds(step * WIDE, 16)] = jnp.concatenate(
                    split(tile), 1
                )

    copies[0].wait()
    prepare(jnp.log(1.0 + count_v[...].astype(F32)).reshape(COLS * ROWS, DEPTH), 0)
    copies[1].wait()
    prepare(field_v.at[0].reshape(COLS * ROWS, DEPTH), 1)
    sweep(0)
    sweep(1)
    for field in range(1, 4):
        copies[field + 1].wait()
        prepare(field_v.at[field].reshape(COLS * ROWS, DEPTH), field + 1)
    for field in range(2, 5):
        sweep(field)
    for first in range(0, 5, 2):
        windows = [(field, BODY // WIDE) for field in range(first, min(first + 2, 5))]
        out = product(windows)
        for j, (field, _) in enumerate(windows):
            last[field] = out[:, j * DEPTH : (j + 1) * DEPTH].reshape(ROWS, WIDE, DEPTH)

    flat_send = send.reshape(40 * ROWS, COLS)
    own_matrix = end_matrix[lax.axis_index("tile") % 2]
    zero = jnp.zeros((8, DEPTH), F32)
    for index in range(20):
        field, pair = index // 4, index % 4
        parts = []
        for j in range(2):
            tail = jnp.concatenate([last[field, pair * 2 + j], zero], 0)
            parts += [bodies[index, j], jnp.concatenate(split(tail), 1)]
        out = depth_product(own_matrix, jnp.concatenate(parts, 0))
        for j in range(2):
            flat_send[pl.ds(field * 64 + pair * 2 + j, 8, stride=ROWS), :] = out[
                :, j * 128 : (j + 1) * 128
            ]
    copies[5].wait()


def depth_product(matrix, stack):
    out = lax.dot_general(
        matrix, stack, (((1,), (1,)), ((), ())), preferred_element_type=F32
    )
    half = matrix.shape[0] // 2
    return out[:half] + out[half:]


def rim_kernel(
    n_tile, table, class_v, last, rim, far, near, rim_matrix, matrix,
    class_t, tables, tails, send,
):
    lane = lax.broadcasted_iota(jnp.int32, (CLASSES, CLASSES), 1)
    row_index = lax.broadcasted_iota(jnp.int32, (CLASSES, CLASSES), 0)
    for channel in range(4):
        scale = 0.5 if channel < 3 else 1.0
        for coefficient in range(6):
            per_class = jnp.broadcast_to(
                table[coefficient, channel : channel + 1, :], (CLASSES, CLASSES)
            )
            column = jnp.sum(
                jnp.where(lane == row_index, per_class, 0.0), axis=1, keepdims=True
            )
            tables[channel * 6 + coefficient] = jnp.broadcast_to(column * scale, (CLASSES, 128))

    flat = class_v.reshape(COLS * ROWS, DEPTH)
    flat_t = class_t.reshape(DEPTH * ROWS, COLS)
    for row in range(ROWS):
        plane = flat[pl.ds(row, COLS, stride=ROWS), :]
        flat_t[pl.ds(row, DEPTH, stride=ROWS), :] = pltpu.roll(plane.T, COLS - RADIUS, 1)

    tile = lax.axis_index("tile")
    even = tile % 2 == 0
    has_left = (tile > 0).astype(F32)
    has_right = (tile < n_tile - 1).astype(F32)
    side = RADIUS * ROWS
    is_right = lax.broadcasted_iota(jnp.int32, (8 * ROWS, DEPTH), 0) % 8 < RADIUS
    edges = []
    for field in range(5):
        from_far = far[field].reshape(side, DEPTH)
        from_near = near[field].reshape(side, DEPTH)
        left = jnp.where(even, from_far, from_near) * has_left
        right = jnp.where(even, from_near, from_far) * has_right
        out = []
        for cells in ([left, rim[field, :64]], [rim[field, 64:], right]):
            parts = split(jnp.concatenate(cells, 0))
            out.append(jnp.concatenate(parts, 0))
        out = plane_blur(rim_matrix, jnp.concatenate(out, 1))
        out = jnp.where(is_right, out[:, DEPTH:], out[:, :DEPTH])
        edges.append(out)
        for row in range(ROWS):
            tail = jnp.concatenate(
                [last[field, row], out[row * 8 : (row + 1) * 8]], 0
            )
            tails[field * 4 + row // 2, row % 2] = jnp.concatenate(split(tail), 1)
    zero = jnp.zeros((64, DEPTH), F32)
    for first in range(0, 5, 2):
        parts = []
        for out in edges[first : first + 2]:
            parts += [out, zero]
        stack = jnp.concatenate(split(jnp.concatenate(parts, 0)), 1)
        out = depth_product(matrix[tile % 2], stack)
        for j in range(stack.shape[0] // 128):
            send[first + j] = out[:, j * 128 : (j + 1) * 128]
    for k in range(RADIUS):
        send[5 + k] = jnp.where(even, class_t[DEPTH - RADIUS + k], class_t[k]).astype(F32)


def shade_cell(values, label, tables, scale, state):
    trans, s_sum, r_sum, g_sum, b_sum, step_sum = state
    linears = []
    for channel in range(4):
        entry = [
            jnp.take_along_axis(
                tables[channel * 6 + i], label, axis=0, mode="promise_in_bounds"
            )
            for i in range(6)
        ]
        linear = entry[0] * values[0] + entry[5]
        for i in range(1, 5):
            linear = linear + entry[i] * values[i]
        linears.append(linear)
    tints = [jnp.tanh(linear) for linear in linears[:3]]
    x = linears[3]
    t = jnp.exp(-jnp.abs(x))
    series = t * (1.0 - t * (1.0 / 2 - t * (1.0 / 3 - t * (1.0 / 4))))
    soft = jnp.maximum(x, 0.0) + jnp.where(t < 0.01, series, jnp.log(1.0 + t))
    step = soft * scale
    opacity = step * (
        1.0 - step * (1.0 / 2 - step * (1.0 / 6 - step * (1.0 / 24 - step * (1.0 / 120))))
    )
    shade = trans * opacity
    return (
        trans - shade,
        s_sum + shade,
        r_sum + shade * tints[0],
        g_sum + shade * tints[1],
        b_sum + shade * tints[2],
        step_sum + step,
    )


def fresh_state():
    zero = jnp.zeros((ROWS, COLS), F32)
    return (jnp.ones((ROWS, COLS), F32), zero, zero, zero, zero, zero)


def join(near, far):
    trans = near[0]
    sums = [near[i] + trans * far[i] for i in range(1, 5)]
    return (trans * far[0], *sums, near[5] + far[5])


def choose(flag, one, other):
    return tuple(jnp.where(flag, a, b) for a, b in zip(one, other))


def inner_kernel(scale, bodies, tails, class_t, tables, matrix, out, halo, end, smooth):
    even = lax.axis_index("tile") % 2 == 0
    depths = len(INNER_TARGETS)
    flat = smooth.reshape(5, depths * ROWS, COLS)
    flat_halo = halo.reshape(5, 8 * ROWS, COLS)
    flat_end = end.reshape(5, RADIUS * ROWS, COLS)

    def blur(index, carry):
        field = index // 4
        pair = index % 4
        stack = jnp.concatenate(
            [bodies[index, 0], tails[index, 0], bodies[index, 1], tails[index, 1]], 0
        )
        product = depth_product(matrix[...], stack)
        front, back = product[:8], product[8 + depths :]
        keep = jnp.where(even, front, back)
        last = jnp.where(even, back[:4], front[4:])
        for j in range(2):
            row = pair * 2 + j
            lanes = slice(j * 128, (j + 1) * 128)
            flat[field, pl.ds(row, depths, stride=ROWS), :] = product[8 : 8 + depths, lanes]
            flat_halo[field, pl.ds(row, 8, stride=ROWS), :] = keep[:, lanes]
            flat_end[field, pl.ds(row, RADIUS, stride=ROWS), :] = last[:, lanes]
        return carry

    lax.fori_loop(0, 20, blur, 0, unroll=10)
    unroll = 12

    def body(index, state):
        for k in range(unroll):
            depth = index * unroll + k
            state = shade_cell(
                [smooth[f, depth] for f in range(5)],
                class_t[RADIUS + depth],
                tables,
                scale,
                state,
            )
        return state

    state = lax.fori_loop(0, depths // unroll, body, fresh_state())
    for i in range(6):
        out[i] = state[i]


def edge_kernel(
    scale, n_slab, halo, end_cells, class_t, tables, inner, place, given, given_rim,
    full, other, mine, total,
):
    slab = lax.axis_index("slab")
    even = lax.axis_index("tile") % 2 == 0
    is_first, is_last = slab == 0, slab == n_slab - 1
    alone = jnp.where(even, is_first, is_last)
    arrived = jnp.where(alone, 0.0, 1.0)
    step_one = jnp.where(jnp.logical_and(even, is_first), 0.0, scale)
    step_two = jnp.where(jnp.logical_and(jnp.logical_not(even), is_last), 0.0, scale)
    step_end = jnp.where(jnp.where(even, is_last, is_first), scale, 0.0)

    shape = (8, ROWS, COLS)
    own_row = lax.broadcasted_iota(jnp.int32, shape, 2) // 8 == lax.broadcasted_iota(
        jnp.int32, shape, 1
    )
    for f in range(5):
        sums = jnp.broadcast_to(given_rim[f][:, None, :], shape)
        sums = jnp.where(own_row, sums, 0.0).reshape(8 * ROWS, COLS)
        moved = jnp.dot(
            jnp.concatenate(split(sums), 1), place[...], preferred_element_type=F32
        ).reshape(shape)
        total[f] = halo[f] + (given[pl.ds(f * 8, 8)] + moved) * arrived

    one = two = end = fresh_state()
    for k in range(RADIUS):
        theirs = given_rim[5 + k].astype(jnp.int32)
        front, back = class_t[k], class_t[DEPTH - RADIUS + k]
        values = [total[f, k] for f in range(5)]
        one = shade_cell(values, jnp.where(even, theirs, back), tables, step_one, one)
        values = [total[f, RADIUS + k] for f in range(5)]
        two = shade_cell(values, jnp.where(even, front, theirs), tables, step_two, two)
        values = [end_cells[f, k] for f in range(5)]
        end = shade_cell(values, jnp.where(even, back, front), tables, step_end, end)
    middle = tuple(inner[i] for i in range(6))

    before = join(end, middle)
    odd_part = join(before, one)
    odd_full = join(odd_part, two)
    even_full = join(join(join(one, two), middle), end)
    all_of_it = choose(even, even_full, odd_full)

    def store(ref, state):
        for i in range(3):
            ref[i] = pltpu.roll(0.5 * (state[1] + state[2 + i]), RADIUS, 1)
        ref[3] = pltpu.roll(jnp.exp(-state[5]), RADIUS, 1)

    store(full, all_of_it)
    store(other, choose(jnp.logical_and(even, slab > 0), one, all_of_it))
    store(mine, choose(even, even_full, odd_part))


def in_vmem(*arrays):
    return tuple(pltpu.with_memory_space_constraint(a, VMEM) for a in arrays)


def in_hbm(*arrays):
    return tuple(pltpu.with_memory_space_constraint(a, pltpu.HBM) for a in arrays)


SPEC = pl.BlockSpec(memory_space=VMEM)
HBM_SPEC = pl.BlockSpec(memory_space=pltpu.HBM)
PARAMS = pltpu.CompilerParams(vmem_limit_bytes=32 * 1024 * 1024)


def cost(microseconds):
    return pl.CostEstimate(
        flops=int(microseconds * 1e9), bytes_accessed=int(microseconds * 3.6e6), transcendentals=0
    )


def permute(value, target):
    n_tile, n_slab = lax.axis_size("tile"), lax.axis_size("slab")
    pairs = []
    for t in range(n_tile):
        for s in range(n_slab):
            to_tile, to_slab = target(t, s)
            pairs.append((t * n_slab + s, to_tile * n_slab + to_slab))
    return lax.ppermute(value, ("tile", "slab"), pairs)


def on_device(counts, fields, class_ids, tf_table):
    n_tile, n_slab = lax.axis_size("tile"), lax.axis_size("slab")
    scale = OPTICAL / (DEPTH * n_slab)

    far, near = pl.pallas_call(
        pack_kernel,
        out_shape=[VMEM((5, RADIUS, ROWS, DEPTH), F32)] * 2,
        in_specs=[HBM_SPEC] * 2,
        out_specs=[SPEC] * 2,
        scratch_shapes=[VMEM((2, RADIUS, ROWS, DEPTH), jnp.int32), pltpu.SemaphoreType.DMA((4,))],
        compiler_params=PARAMS,
        cost_estimate=cost(1),
        name="pack",
    )(*in_hbm(counts, fields))

    def across(t, s):
        other = ((t + 1) ^ 1) - 1
        return (other, s) if 0 <= other < n_tile else (t, s ^ 1)

    far = permute(far, across)
    near = lax.ppermute(near, "tile", [(t, t ^ 1) for t in range(n_tile)])

    step_matrix = plane_matrix(list(range(RADIUS, RADIUS + WIDE)), list(range(2 * WIDE)))
    end_matrix = jnp.asarray(np.stack([depth_matrix(BACK_TARGETS), depth_matrix(FRONT_TARGETS)]))
    bodies, last, rim, class_v, send = pl.pallas_call(
        columns_kernel,
        out_shape=[
            VMEM((20, 2, BODY, 2 * DEPTH), BF16),
            VMEM((5, ROWS, WIDE, DEPTH), F32),
            VMEM((5, 16 * ROWS, DEPTH), F32),
            VMEM((COLS, ROWS, DEPTH), jnp.int32),
            VMEM((40, ROWS, COLS), F32),
        ],
        in_specs=[SPEC] * 2 + [HBM_SPEC] * 3,
        out_specs=[SPEC] * 5,
        scratch_shapes=[
            VMEM((COLS, ROWS, DEPTH), jnp.int32),
            VMEM((4, COLS, ROWS, DEPTH), F32),
            VMEM((5, COLS * ROWS, DEPTH), BF16),
            VMEM((5, COLS * ROWS, DEPTH), BF16),
            pltpu.SemaphoreType.DMA((6,)),
        ],
        compiler_params=PARAMS,
        cost_estimate=cost(3),
        name="columns",
    )(*in_vmem(jnp.asarray(step_matrix), end_matrix), *in_hbm(counts, fields, class_ids))

    def beside(t, s):
        to = s + 1 if t % 2 == 0 else s - 1
        return (t, to) if 0 <= to < n_slab else (t ^ 1, s)

    given = permute(send, beside)

    rim_matrix = plane_matrix(2 * list(range(RADIUS, 2 * RADIUS)), list(range(3 * RADIUS)))
    class_t, tables, tails, send_rim = pl.pallas_call(
        functools.partial(rim_kernel, n_tile),
        out_shape=[
            VMEM((DEPTH, ROWS, COLS), jnp.int32),
            VMEM((24, ROWS, 128), F32),
            VMEM((20, 2, COLS - BODY, 2 * DEPTH), BF16),
            VMEM((9, 8, 128), F32),
        ],
        in_specs=[SPEC] * 8,
        out_specs=[SPEC] * 4,
        compiler_params=PARAMS,
        cost_estimate=cost(1),
        name="rim",
    )(
        *in_vmem(
            jnp.transpose(tf_table, (2, 1, 0)), class_v, last, rim, far, near,
            jnp.asarray(rim_matrix), end_matrix,
        )
    )
    given_rim = permute(send_rim, beside)

    depths = len(INNER_TARGETS)
    inner, halo, end_cells = pl.pallas_call(
        functools.partial(inner_kernel, scale),
        out_shape=[
            VMEM((6, ROWS, COLS), F32),
            VMEM((5, 8, ROWS, COLS), F32),
            VMEM((5, RADIUS, ROWS, COLS), F32),
        ],
        in_specs=[SPEC] * 5,
        out_specs=[SPEC] * 3,
        scratch_shapes=[VMEM((5, depths, ROWS, COLS), F32)],
        compiler_params=PARAMS,
        cost_estimate=cost(3.5),
        name="inner",
    )(
        *in_vmem(
            bodies, tails, class_t, tables,
            jnp.asarray(depth_matrix(FRONT_TARGETS + INNER_TARGETS + BACK_TARGETS)),
        )
    )

    place = np.zeros((2, COLS, COLS), np.float32)
    for lane in range(64):
        place[:, lane, INNER + lane % 8] = 1.0
    full, other, mine = pl.pallas_call(
        functools.partial(edge_kernel, scale, n_slab),
        out_shape=[VMEM((4, ROWS, COLS), F32)] * 3,
        in_specs=[SPEC] * 8,
        out_specs=[SPEC] * 3,
        scratch_shapes=[VMEM((5, 8, ROWS, COLS), F32)],
        compiler_params=PARAMS,
        cost_estimate=cost(0.5),
        name="edges",
    )(
        *in_vmem(
            halo, end_cells, class_t, tables, inner,
            jnp.asarray(place.reshape(2 * COLS, COLS), BF16), given, given_rim,
        )
    )

    slab = lax.axis_index("slab")
    even = lax.axis_index("tile") % 2 == 0
    from_2, from_1, from_3 = (
        permute(full, lambda t, s: (t, (2, 3, 1, 0)[s])),
        permute(full, lambda t, s: (t, (s + 1) % n_slab)),
        permute(other, lambda t, s: (t, (s + 3) % n_slab)),
    )

    def only(flag, value):
        return jnp.where(flag, value[:3], 0.0), jnp.where(flag, value[3], 1.0)

    def over(near, far):
        return near[1] * far[0] + near[0], near[1] * far[1]

    last = slab == n_slab - 1
    seen = over(only(slab >= 2, from_2), only(slab >= 1, from_1))
    seen = over(seen, (mine[:3], mine[3]))
    seen = over(seen, only(jnp.logical_and(even, jnp.logical_not(last)), from_3))
    seen = over(only(last, from_3), seen)
    return jnp.concatenate([seen[0], (1.0 - seen[1])[None]], 0)[None]


def solution(mesh):
    return jax.shard_map(
        on_device,
        mesh=mesh,
        in_specs=(
            P("tile", None, "slab"),
            P(None, "tile", None, "slab"),
            P("tile", None, "slab"),
            P(),
        ),
        out_specs=P("slab", None, None, "tile"),
        check_vma=False,
    )
```

```python
import functools
import math

import jax
import jax.numpy as jnp
import numpy as np
from jax import lax
from jax.experimental import pallas as pl
from jax.experimental.pallas import tpu as pltpu
from jax.sharding import PartitionSpec as P

CLASSES = 8
RADIUS = 4
SPLAT = 2.0
OPTICAL = 0.5
COLS, ROWS, DEPTH = 128, 8, 128
F32, BF16 = jnp.float32, jnp.bfloat16
VMEM = pltpu.VMEM


def splat_taps():
    raw = [
        math.exp(-((offset - RADIUS) ** 2) / (2.0 * SPLAT * SPLAT))
        for offset in range(2 * RADIUS + 1)
    ]
    norm_total = sum(raw)
    return [value / norm_total for value in raw]


W = splat_taps()


def shades_forward(tile):
    return tile % 2 == 1


def tap(offset):
    return W[offset + RADIUS] if abs(offset) <= RADIUS else 0.0


def split_const(full):
    high = full.astype(jnp.bfloat16)
    return high, (full - high.astype(np.float64)).astype(jnp.bfloat16)


def split_rows(full):
    high, low = split_const(full)
    top = np.concatenate([high, high], 1)
    bottom = np.concatenate([low, np.zeros_like(low)], 1)
    return np.concatenate([top, bottom], 0)


def depth_matrix(targets):
    return split_rows(
        np.array([[tap(cell - target) for cell in range(DEPTH)] for target in targets])
    )


def plane_matrix(targets, cells):
    full = np.zeros((ROWS, len(targets), len(cells), ROWS), np.float64)
    for to_row in range(ROWS):
        for i, target in enumerate(targets):
            for j, cell in enumerate(cells):
                for row in range(ROWS):
                    full[to_row, i, j, row] = tap(cell - target) * tap(row - to_row)
    return split_rows(full.reshape(ROWS * len(targets), len(cells) * ROWS))


WIDE = 8
INNER = COLS - 2 * RADIUS
FRONT_TARGETS = list(range(-RADIUS, RADIUS))
INNER_TARGETS = list(range(RADIUS, DEPTH - RADIUS))
BACK_TARGETS = list(range(DEPTH - RADIUS, DEPTH + RADIUS))
BODY = 112


def split(value):
    high = value.astype(BF16)
    return high, (value - high.astype(F32)).astype(BF16)


def plane_blur(matrix, stack):
    out = jnp.dot(matrix[...], stack, preferred_element_type=F32)
    rows = matrix.shape[0] // 2
    return out[:rows] + out[rows:]


def pack_kernel(counts, fields, far, near, count_rows, sems):
    even = lax.axis_index("tile") % 2 == 0
    copies = []
    for i, (ref, at_start) in enumerate(((far, even), (near, jnp.logical_not(even)))):
        cells = pl.ds(jnp.where(at_start, 0, COLS - RADIUS), RADIUS)
        copies.append(pltpu.make_async_copy(counts.at[cells], count_rows.at[i], sems.at[2 * i]))
        copies.append(
            pltpu.make_async_copy(fields.at[:, cells], ref.at[pl.ds(1, 4)], sems.at[2 * i + 1])
        )
    for copy in copies:
        copy.start()
    for copy in copies:
        copy.wait()
    far[0] = jnp.log(1.0 + count_rows[0].astype(F32))
    near[0] = jnp.log(1.0 + count_rows[1].astype(F32))


def columns_kernel(
    matrix, end_matrix, counts, fields, classes,
    bodies, last, rim, class_v, send,
    count_v, field_v, high, low, sems,
):
    copies = [pltpu.make_async_copy(counts, count_v, sems.at[0])]
    for field in range(4):
        copies.append(
            pltpu.make_async_copy(fields.at[field], field_v.at[field], sems.at[field + 1])
        )
    copies.append(pltpu.make_async_copy(classes, class_v, sems.at[5]))
    for copy in copies:
        copy.start()

    def prepare(source, field):
        rim[field, pl.ds(0, 64), :] = source[pl.ds(0, 64), :]
        rim[field, pl.ds(64, 64), :] = source[pl.ds((COLS - 8) * ROWS, 64), :]
        high[field], low[field] = split(source[...])

    def product(windows):
        sides = []
        for field, step in windows:
            cells = pl.ds(step * WIDE * ROWS, 2 * WIDE * ROWS)
            sides.append(jnp.concatenate([high[field, cells, :], low[field, cells, :]], 0))
        return plane_blur(matrix, jnp.concatenate(sides, 1))

    def sweep(field):
        for step in range(0, BODY // WIDE, 2):
            out = product([(field, step), (field, step + 1)])
            for row in range(ROWS):
                cut = out[row * WIDE : (row + 1) * WIDE]
                tile = jnp.concatenate([cut[:, :DEPTH], cut[:, DEPTH:]], 0)
                bodies[field * 4 + row // 2, row % 2, pl.ds(step * WIDE, 16)] = jnp.concatenate(
                    split(tile), 1
                )

    copies[0].wait()
    prepare(jnp.log(1.0 + count_v[...].astype(F32)).reshape(COLS * ROWS, DEPTH), 0)
    copies[1].wait()
    prepare(field_v.at[0].reshape(COLS * ROWS, DEPTH), 1)
    sweep(0)
    sweep(1)
    for field in range(1, 4):
        copies[field + 1].wait()
        prepare(field_v.at[field].reshape(COLS * ROWS, DEPTH), field + 1)
    for field in range(2, 5):
        sweep(field)
    for first in range(0, 5, 2):
        windows = [(field, BODY // WIDE) for field in range(first, min(first + 2, 5))]
        out = product(windows)
        for j, (field, _) in enumerate(windows):
            last[field] = out[:, j * DEPTH : (j + 1) * DEPTH].reshape(ROWS, WIDE, DEPTH)

    flat_send = send.reshape(40 * ROWS, COLS)
    own_matrix = end_matrix[jnp.where(shades_forward(lax.axis_index("tile")), 0, 1)]
    zero = jnp.zeros((8, DEPTH), F32)
    for index in range(20):
        field, pair = index // 4, index % 4
        parts = []
        for j in range(2):
            tail = jnp.concatenate([last[field, pair * 2 + j], zero], 0)
            parts += [bodies[index, j], jnp.concatenate(split(tail), 1)]
        out = depth_product(own_matrix, jnp.concatenate(parts, 0))
        for j in range(2):
            flat_send[pl.ds(field * 64 + pair * 2 + j, 8, stride=ROWS), :] = out[
                :, j * 128 : (j + 1) * 128
            ]
    copies[5].wait()


def depth_product(matrix, stack):
    out = lax.dot_general(
        matrix, stack, (((1,), (1,)), ((), ())), preferred_element_type=F32
    )
    half = matrix.shape[0] // 2
    return out[:half] + out[half:]


def rim_kernel(
    n_tile, table, class_v, last, rim, far, near, rim_matrix, matrix,
    class_t, tables, tails, send,
):
    lane = lax.broadcasted_iota(jnp.int32, (CLASSES, CLASSES), 1)
    row_index = lax.broadcasted_iota(jnp.int32, (CLASSES, CLASSES), 0)
    for channel in range(4):
        scale = 0.5 if channel < 3 else 1.0
        for coefficient in range(6):
            per_class = jnp.broadcast_to(
                table[coefficient, channel : channel + 1, :], (CLASSES, CLASSES)
            )
            column = jnp.sum(
                jnp.where(lane == row_index, per_class, 0.0), axis=1, keepdims=True
            )
            tables[channel * 6 + coefficient] = jnp.broadcast_to(column * scale, (CLASSES, 128))

    flat = class_v.reshape(COLS * ROWS, DEPTH)
    flat_t = class_t.reshape(DEPTH * ROWS, COLS)
    for row in range(ROWS):
        plane = flat[pl.ds(row, COLS, stride=ROWS), :]
        flat_t[pl.ds(row, DEPTH, stride=ROWS), :] = pltpu.roll(plane.T, COLS - RADIUS, 1)

    tile = lax.axis_index("tile")
    even = tile % 2 == 0
    forward = shades_forward(tile)
    has_left = (tile > 0).astype(F32)
    has_right = (tile < n_tile - 1).astype(F32)
    side = RADIUS * ROWS
    is_right = lax.broadcasted_iota(jnp.int32, (8 * ROWS, DEPTH), 0) % 8 < RADIUS
    edges = []
    for field in range(5):
        from_far = far[field].reshape(side, DEPTH)
        from_near = near[field].reshape(side, DEPTH)
        left = jnp.where(even, from_far, from_near) * has_left
        right = jnp.where(even, from_near, from_far) * has_right
        out = []
        for cells in ([left, rim[field, :64]], [rim[field, 64:], right]):
            parts = split(jnp.concatenate(cells, 0))
            out.append(jnp.concatenate(parts, 0))
        out = plane_blur(rim_matrix, jnp.concatenate(out, 1))
        out = jnp.where(is_right, out[:, DEPTH:], out[:, :DEPTH])
        edges.append(out)
        for row in range(ROWS):
            tail = jnp.concatenate(
                [last[field, row], out[row * 8 : (row + 1) * 8]], 0
            )
            tails[field * 4 + row // 2, row % 2] = jnp.concatenate(split(tail), 1)
    zero = jnp.zeros((64, DEPTH), F32)
    for first in range(0, 5, 2):
        parts = []
        for out in edges[first : first + 2]:
            parts += [out, zero]
        stack = jnp.concatenate(split(jnp.concatenate(parts, 0)), 1)
        out = depth_product(matrix[jnp.where(forward, 0, 1)], stack)
        for j in range(stack.shape[0] // 128):
            send[first + j] = out[:, j * 128 : (j + 1) * 128]
    for k in range(RADIUS):
        send[5 + k] = jnp.where(forward, class_t[DEPTH - RADIUS + k], class_t[k]).astype(F32)


def shade_cell(values, label, tables, scale, state):
    trans, s_sum, r_sum, g_sum, b_sum, step_sum = state
    linears = []
    for channel in range(4):
        entry = [
            jnp.take_along_axis(
                tables[channel * 6 + i], label, axis=0, mode="promise_in_bounds"
            )
            for i in range(6)
        ]
        linear = entry[0] * values[0] + entry[5]
        for i in range(1, 5):
            linear = linear + entry[i] * values[i]
        linears.append(linear)
    tints = [jnp.tanh(linear) for linear in linears[:3]]
    x = linears[3]
    t = jnp.exp(-jnp.abs(x))
    series = t * (1.0 - t * (1.0 / 2 - t * (1.0 / 3 - t * (1.0 / 4))))
    soft = jnp.maximum(x, 0.0) + jnp.where(t < 0.01, series, jnp.log(1.0 + t))
    step = soft * scale
    opacity = step * (
        1.0 - step * (1.0 / 2 - step * (1.0 / 6 - step * (1.0 / 24 - step * (1.0 / 120))))
    )
    shade = trans * opacity
    return (
        trans - shade,
        s_sum + shade,
        r_sum + shade * tints[0],
        g_sum + shade * tints[1],
        b_sum + shade * tints[2],
        step_sum + step,
    )


def fresh_state():
    zero = jnp.zeros((ROWS, COLS), F32)
    return (jnp.ones((ROWS, COLS), F32), zero, zero, zero, zero, zero)


def join(near, far):
    trans = near[0]
    sums = [near[i] + trans * far[i] for i in range(1, 5)]
    return (trans * far[0], *sums, near[5] + far[5])


def choose(flag, one, other):
    return tuple(jnp.where(flag, a, b) for a, b in zip(one, other))


def inner_kernel(scale, bodies, tails, class_t, tables, matrix, out, halo, end, smooth):
    forward = shades_forward(lax.axis_index("tile"))
    depths = len(INNER_TARGETS)
    flat = smooth.reshape(5, depths * ROWS, COLS)
    flat_halo = halo.reshape(5, 8 * ROWS, COLS)
    flat_end = end.reshape(5, RADIUS * ROWS, COLS)

    def blur(index, carry):
        field = index // 4
        pair = index % 4
        stack = jnp.concatenate(
            [bodies[index, 0], tails[index, 0], bodies[index, 1], tails[index, 1]], 0
        )
        product = depth_product(matrix[...], stack)
        front, back = product[:8], product[8 + depths :]
        keep = jnp.where(forward, front, back)
        last = jnp.where(forward, back[:4], front[4:])
        for j in range(2):
            row = pair * 2 + j
            lanes = slice(j * 128, (j + 1) * 128)
            flat[field, pl.ds(row, depths, stride=ROWS), :] = product[8 : 8 + depths, lanes]
            flat_halo[field, pl.ds(row, 8, stride=ROWS), :] = keep[:, lanes]
            flat_end[field, pl.ds(row, RADIUS, stride=ROWS), :] = last[:, lanes]
        return carry

    lax.fori_loop(0, 20, blur, 0, unroll=10)
    unroll = 12

    def body(index, state):
        for k in range(unroll):
            depth = index * unroll + k
            state = shade_cell(
                [smooth[f, depth] for f in range(5)],
                class_t[RADIUS + depth],
                tables,
                scale,
                state,
            )
        return state

    state = lax.fori_loop(0, depths // unroll, body, fresh_state())
    for i in range(6):
        out[i] = state[i]


def edge_kernel(
    scale, n_slab, halo, end_cells, class_t, tables, inner, place, given, given_rim,
    full, to_two, to_three, mine, total,
):
    slab = lax.axis_index("slab")
    forward = shades_forward(lax.axis_index("tile"))
    is_first, is_last = slab == 0, slab == n_slab - 1
    alone = jnp.where(forward, is_first, is_last)
    arrived = jnp.where(alone, 0.0, 1.0)
    step_one = jnp.where(jnp.logical_and(forward, is_first), 0.0, scale)
    step_two = jnp.where(jnp.logical_and(jnp.logical_not(forward), is_last), 0.0, scale)
    step_end = jnp.where(jnp.where(forward, is_last, is_first), scale, 0.0)

    shape = (8, ROWS, COLS)
    own_row = lax.broadcasted_iota(jnp.int32, shape, 2) // 8 == lax.broadcasted_iota(
        jnp.int32, shape, 1
    )
    for f in range(5):
        sums = jnp.broadcast_to(given_rim[f][:, None, :], shape)
        sums = jnp.where(own_row, sums, 0.0).reshape(8 * ROWS, COLS)
        moved = jnp.dot(
            jnp.concatenate(split(sums), 1), place[...], preferred_element_type=F32
        ).reshape(shape)
        total[f] = halo[f] + (given[pl.ds(f * 8, 8)] + moved) * arrived

    one = two = end = fresh_state()
    for k in range(RADIUS):
        theirs = given_rim[5 + k].astype(jnp.int32)
        front, back = class_t[k], class_t[DEPTH - RADIUS + k]
        values = [total[f, k] for f in range(5)]
        one = shade_cell(values, jnp.where(forward, theirs, back), tables, step_one, one)
        values = [total[f, RADIUS + k] for f in range(5)]
        two = shade_cell(values, jnp.where(forward, front, theirs), tables, step_two, two)
        values = [end_cells[f, k] for f in range(5)]
        end = shade_cell(values, jnp.where(forward, back, front), tables, step_end, end)
    middle = tuple(inner[i] for i in range(6))

    before = join(end, middle)
    backward_part = join(before, one)
    backward_full = join(backward_part, two)
    forward_full = join(join(join(one, two), middle), end)
    all_of_it = choose(forward, forward_full, backward_full)

    def store(ref, state):
        for i in range(3):
            ref[i] = pltpu.roll(0.5 * (state[1] + state[2 + i]), RADIUS, 1)
        ref[3] = pltpu.roll(jnp.exp(-state[5]), RADIUS, 1)

    store(full, all_of_it)
    store(to_two, choose(jnp.logical_and(forward, slab % 2 == 1), one, all_of_it))
    store(to_three, choose(jnp.logical_and(forward, slab >= 2), one, all_of_it))
    store(mine, choose(forward, forward_full, backward_part))


def pair(ref):
    return [ref[i] for i in range(4)]


def over(near, far):
    return [near[i] + near[3] * far[i] for i in range(3)] + [near[3] * far[3]]


def only(flag, value):
    return [jnp.where(flag, value[i], 0.0) for i in range(3)] + [jnp.where(flag, value[3], 1.0)]


def final_kernel(got_one, got_two, got_three, mine, out):
    slab = lax.axis_index("slab")
    forward = shades_forward(lax.axis_index("tile"))
    by_one, by_two, by_three = pair(got_one), pair(got_two), pair(got_three)
    total = only(slab == 3, by_one)
    total = over(total, only(slab >= 2, by_three))
    total = over(total, only(jnp.logical_and(forward, slab == 2), by_one))
    total = over(total, only(jnp.where(forward, slab % 2 == 1, slab >= 1), by_two))
    total = over(total, pair(mine))
    total = over(total, only(jnp.logical_and(forward, slab % 2 == 0), by_two))
    total = over(total, only(jnp.logical_and(forward, slab == 1), by_three))
    for i in range(3):
        out[0, i] = total[i]
    out[0, 3] = 1.0 - total[3]


def in_vmem(*arrays):
    return tuple(pltpu.with_memory_space_constraint(a, VMEM) for a in arrays)


def in_hbm(*arrays):
    return tuple(pltpu.with_memory_space_constraint(a, pltpu.HBM) for a in arrays)


SPEC = pl.BlockSpec(memory_space=VMEM)
HBM_SPEC = pl.BlockSpec(memory_space=pltpu.HBM)
PARAMS = pltpu.CompilerParams(vmem_limit_bytes=32 * 1024 * 1024)


def cost(microseconds):
    return pl.CostEstimate(
        flops=int(microseconds * 1e9), bytes_accessed=int(microseconds * 3.6e6), transcendentals=0
    )


def permute(value, target):
    n_tile, n_slab = lax.axis_size("tile"), lax.axis_size("slab")
    pairs = []
    for t in range(n_tile):
        for s in range(n_slab):
            to_tile, to_slab = target(t, s)
            pairs.append((t * n_slab + s, to_tile * n_slab + to_slab))
    return lax.ppermute(value, ("tile", "slab"), pairs)


def on_device(counts, fields, class_ids, tf_table):
    n_tile, n_slab = lax.axis_size("tile"), lax.axis_size("slab")
    scale = OPTICAL / (DEPTH * n_slab)

    far, near = pl.pallas_call(
        pack_kernel,
        out_shape=[VMEM((5, RADIUS, ROWS, DEPTH), F32)] * 2,
        in_specs=[HBM_SPEC] * 2,
        out_specs=[SPEC] * 2,
        scratch_shapes=[VMEM((2, RADIUS, ROWS, DEPTH), jnp.int32), pltpu.SemaphoreType.DMA((4,))],
        compiler_params=PARAMS,
        cost_estimate=cost(1),
        name="pack",
    )(*in_hbm(counts, fields))

    def across(t, s):
        other = ((t + 1) ^ 1) - 1
        return (other, s) if 0 <= other < n_tile else (t, s ^ 1)

    far = permute(far, across)
    near = lax.ppermute(near, "tile", [(t, t ^ 1) for t in range(n_tile)])

    step_matrix = plane_matrix(list(range(RADIUS, RADIUS + WIDE)), list(range(2 * WIDE)))
    end_matrix = jnp.asarray(np.stack([depth_matrix(BACK_TARGETS), depth_matrix(FRONT_TARGETS)]))
    bodies, last, rim, class_v, send = pl.pallas_call(
        columns_kernel,
        out_shape=[
            VMEM((20, 2, BODY, 2 * DEPTH), BF16),
            VMEM((5, ROWS, WIDE, DEPTH), F32),
            VMEM((5, 16 * ROWS, DEPTH), F32),
            VMEM((COLS, ROWS, DEPTH), jnp.int32),
            VMEM((40, ROWS, COLS), F32),
        ],
        in_specs=[SPEC] * 2 + [HBM_SPEC] * 3,
        out_specs=[SPEC] * 5,
        scratch_shapes=[
            VMEM((COLS, ROWS, DEPTH), jnp.int32),
            VMEM((4, COLS, ROWS, DEPTH), F32),
            VMEM((5, COLS * ROWS, DEPTH), BF16),
            VMEM((5, COLS * ROWS, DEPTH), BF16),
            pltpu.SemaphoreType.DMA((6,)),
        ],
        compiler_params=PARAMS,
        cost_estimate=cost(3),
        name="columns",
    )(*in_vmem(jnp.asarray(step_matrix), end_matrix), *in_hbm(counts, fields, class_ids))

    def beside(t, s):
        to = s + 1 if shades_forward(t) else s - 1
        return (t, to) if 0 <= to < n_slab else (t ^ 1, s)

    given = permute(send, beside)

    rim_matrix = plane_matrix(2 * list(range(RADIUS, 2 * RADIUS)), list(range(3 * RADIUS)))
    class_t, tables, tails, send_rim = pl.pallas_call(
        functools.partial(rim_kernel, n_tile),
        out_shape=[
            VMEM((DEPTH, ROWS, COLS), jnp.int32),
            VMEM((24, ROWS, 128), F32),
            VMEM((20, 2, COLS - BODY, 2 * DEPTH), BF16),
            VMEM((9, 8, 128), F32),
        ],
        in_specs=[SPEC] * 8,
        out_specs=[SPEC] * 4,
        compiler_params=PARAMS,
        cost_estimate=cost(1),
        name="rim",
    )(
        *in_vmem(
            jnp.transpose(tf_table, (2, 1, 0)), class_v, last, rim, far, near,
            jnp.asarray(rim_matrix), end_matrix,
        )
    )
    given_rim = permute(send_rim, beside)

    depths = len(INNER_TARGETS)
    inner, halo, end_cells = pl.pallas_call(
        functools.partial(inner_kernel, scale),
        out_shape=[
            VMEM((6, ROWS, COLS), F32),
            VMEM((5, 8, ROWS, COLS), F32),
            VMEM((5, RADIUS, ROWS, COLS), F32),
        ],
        in_specs=[SPEC] * 5,
        out_specs=[SPEC] * 3,
        scratch_shapes=[VMEM((5, depths, ROWS, COLS), F32)],
        compiler_params=PARAMS,
        cost_estimate=cost(3.5),
        name="inner",
    )(
        *in_vmem(
            bodies, tails, class_t, tables,
            jnp.asarray(depth_matrix(FRONT_TARGETS + INNER_TARGETS + BACK_TARGETS)),
        )
    )

    place = np.zeros((2, COLS, COLS), np.float32)
    for lane in range(64):
        place[:, lane, INNER + lane % 8] = 1.0
    full, to_two, to_three, mine = pl.pallas_call(
        functools.partial(edge_kernel, scale, n_slab),
        out_shape=[VMEM((4, ROWS, COLS), F32)] * 4,
        in_specs=[SPEC] * 8,
        out_specs=[SPEC] * 4,
        scratch_shapes=[VMEM((5, 8, ROWS, COLS), F32)],
        compiler_params=PARAMS,
        cost_estimate=cost(0.5),
        name="edges",
    )(
        *in_vmem(
            halo, end_cells, class_t, tables, inner,
            jnp.asarray(place.reshape(2 * COLS, COLS), BF16), given, given_rim,
        )
    )

    def first(t, s):
        if shades_forward(t):
            return ((t, 3), (t, 2), (t ^ 1, 2), (t, 0))[s]
        return ((t, 3), (t ^ 1, 1), (t, 1), (t, 0))[s]

    def second(t, s):
        return (t, s ^ 1 if shades_forward(t) else (s + 1) % n_slab)

    got_one = permute(full, first)
    got_two = permute(to_two, second)
    got_three = permute(to_three, lambda t, s: (t, (2, 3, 1, 0)[s]))
    return pl.pallas_call(
        final_kernel,
        out_shape=jax.ShapeDtypeStruct((1, 4, ROWS, COLS), F32),
        in_specs=[SPEC] * 4,
        out_specs=SPEC,
        compiler_params=PARAMS,
        name="final",
    )(*in_vmem(got_one, got_two, got_three, mine))


def solution(mesh):
    return jax.shard_map(
        on_device,
        mesh=mesh,
        in_specs=(
            P("tile", None, "slab"),
            P(None, "tile", None, "slab"),
            P("tile", None, "slab"),
            P(),
        ),
        out_specs=P("slab", None, None, "tile"),
        check_vma=False,
    )
```

```python
import functools
import math

import jax
import jax.numpy as jnp
import numpy as np
from jax import lax
from jax.experimental import pallas as pl
from jax.experimental.pallas import tpu as pltpu
from jax.sharding import PartitionSpec as P

CLASSES = 8
RADIUS = 4
SPLAT = 2.0
OPTICAL = 0.5
COLS, ROWS, DEPTH = 128, 8, 128
F32, BF16 = jnp.float32, jnp.bfloat16
VMEM = pltpu.VMEM


def splat_taps():
    raw = [
        math.exp(-((offset - RADIUS) ** 2) / (2.0 * SPLAT * SPLAT))
        for offset in range(2 * RADIUS + 1)
    ]
    norm_total = sum(raw)
    return [value / norm_total for value in raw]


W = splat_taps()


def shades_forward(tile):
    return tile % 2 == 1


def tap(offset):
    return W[offset + RADIUS] if abs(offset) <= RADIUS else 0.0


def split_const(full):
    high = full.astype(jnp.bfloat16)
    return high, (full - high.astype(np.float64)).astype(jnp.bfloat16)


def split_rows(full):
    high, low = split_const(full)
    top = np.concatenate([high, high], 1)
    bottom = np.concatenate([low, np.zeros_like(low)], 1)
    return np.concatenate([top, bottom], 0)


def depth_matrix(targets):
    return split_rows(
        np.array([[tap(cell - target) for cell in range(DEPTH)] for target in targets])
    )


def plane_matrix(targets, cells):
    full = np.zeros((ROWS, len(targets), len(cells), ROWS), np.float64)
    for to_row in range(ROWS):
        for i, target in enumerate(targets):
            for j, cell in enumerate(cells):
                for row in range(ROWS):
                    full[to_row, i, j, row] = tap(cell - target) * tap(row - to_row)
    return split_rows(full.reshape(ROWS * len(targets), len(cells) * ROWS))


WIDE = 8
INNER = COLS - 2 * RADIUS
FRONT_TARGETS = list(range(-RADIUS, RADIUS))
INNER_TARGETS = list(range(RADIUS, DEPTH - RADIUS))
BACK_TARGETS = list(range(DEPTH - RADIUS, DEPTH + RADIUS))
BODY = 112


def split(value):
    high = value.astype(BF16)
    return high, (value - high.astype(F32)).astype(BF16)


def plane_blur(matrix, stack):
    out = jnp.dot(matrix[...], stack, preferred_element_type=F32)
    rows = matrix.shape[0] // 2
    return out[:rows] + out[rows:]


def pack_kernel(counts, fields, far, near, count_rows, sems):
    even = lax.axis_index("tile") % 2 == 0
    copies = []
    for i, (ref, at_start) in enumerate(((far, even), (near, jnp.logical_not(even)))):
        cells = pl.ds(jnp.where(at_start, 0, COLS - RADIUS), RADIUS)
        copies.append(pltpu.make_async_copy(counts.at[cells], count_rows.at[i], sems.at[2 * i]))
        copies.append(
            pltpu.make_async_copy(fields.at[:, cells], ref.at[pl.ds(1, 4)], sems.at[2 * i + 1])
        )
    for copy in copies:
        copy.start()
    for copy in copies:
        copy.wait()
    far[0] = jnp.log(1.0 + count_rows[0].astype(F32))
    near[0] = jnp.log(1.0 + count_rows[1].astype(F32))


def columns_kernel(
    matrix, end_matrix, count_v, field_v,
    bodies, last, rim, send,
    high, low,
):
    def prepare(source, field):
        rim[field, pl.ds(0, 64), :] = source[pl.ds(0, 64), :]
        rim[field, pl.ds(64, 64), :] = source[pl.ds((COLS - 8) * ROWS, 64), :]
        high[field], low[field] = split(source[...])

    def product(windows):
        sides = []
        for field, step in windows:
            cells = pl.ds(step * WIDE * ROWS, 2 * WIDE * ROWS)
            sides.append(jnp.concatenate([high[field, cells, :], low[field, cells, :]], 0))
        return plane_blur(matrix, jnp.concatenate(sides, 1))

    def sweep(field):
        for step in range(0, BODY // WIDE, 2):
            out = product([(field, step), (field, step + 1)])
            for row in range(ROWS):
                cut = out[row * WIDE : (row + 1) * WIDE]
                tile = jnp.concatenate([cut[:, :DEPTH], cut[:, DEPTH:]], 0)
                bodies[field * 4 + row // 2, row % 2, pl.ds(step * WIDE, 16)] = jnp.concatenate(
                    split(tile), 1
                )

    prepare(jnp.log(1.0 + count_v[...].astype(F32)).reshape(COLS * ROWS, DEPTH), 0)
    prepare(field_v.at[0].reshape(COLS * ROWS, DEPTH), 1)
    sweep(0)
    sweep(1)
    for field in range(1, 4):
        prepare(field_v.at[field].reshape(COLS * ROWS, DEPTH), field + 1)
    for field in range(2, 5):
        sweep(field)
    for first in range(0, 5, 2):
        windows = [(field, BODY // WIDE) for field in range(first, min(first + 2, 5))]
        out = product(windows)
        for j, (field, _) in enumerate(windows):
            last[field] = out[:, j * DEPTH : (j + 1) * DEPTH].reshape(ROWS, WIDE, DEPTH)

    flat_send = send.reshape(40 * ROWS, COLS)
    own_matrix = end_matrix[jnp.where(shades_forward(lax.axis_index("tile")), 0, 1)]
    zero = jnp.zeros((8, DEPTH), F32)
    for index in range(20):
        field, pair = index // 4, index % 4
        parts = []
        for j in range(2):
            tail = jnp.concatenate([last[field, pair * 2 + j], zero], 0)
            parts += [bodies[index, j], jnp.concatenate(split(tail), 1)]
        out = depth_product(own_matrix, jnp.concatenate(parts, 0))
        for j in range(2):
            flat_send[pl.ds(field * 64 + pair * 2 + j, 8, stride=ROWS), :] = out[
                :, j * 128 : (j + 1) * 128
            ]


def depth_product(matrix, stack):
    out = lax.dot_general(
        matrix, stack, (((1,), (1,)), ((), ())), preferred_element_type=F32
    )
    half = matrix.shape[0] // 2
    return out[:half] + out[half:]


def rim_kernel(
    n_tile, table, class_v, last, rim, far, near, rim_matrix, matrix,
    class_t, tables, tails, send,
):
    lane = lax.broadcasted_iota(jnp.int32, (CLASSES, CLASSES), 1)
    row_index = lax.broadcasted_iota(jnp.int32, (CLASSES, CLASSES), 0)
    for channel in range(4):
        scale = 0.5 if channel < 3 else 1.0
        for coefficient in range(6):
            per_class = jnp.broadcast_to(
                table[coefficient, channel : channel + 1, :], (CLASSES, CLASSES)
            )
            column = jnp.sum(
                jnp.where(lane == row_index, per_class, 0.0), axis=1, keepdims=True
            )
            tables[channel * 6 + coefficient] = jnp.broadcast_to(column * scale, (CLASSES, 128))

    flat = class_v.reshape(COLS * ROWS, DEPTH)
    flat_t = class_t.reshape(DEPTH * ROWS, COLS)
    for row in range(ROWS):
        plane = flat[pl.ds(row, COLS, stride=ROWS), :]
        flat_t[pl.ds(row, DEPTH, stride=ROWS), :] = pltpu.roll(plane.T, COLS - RADIUS, 1)

    tile = lax.axis_index("tile")
    even = tile % 2 == 0
    forward = shades_forward(tile)
    has_left = (tile > 0).astype(F32)
    has_right = (tile < n_tile - 1).astype(F32)
    side = RADIUS * ROWS
    is_right = lax.broadcasted_iota(jnp.int32, (8 * ROWS, DEPTH), 0) % 8 < RADIUS
    edges = []
    for field in range(5):
        from_far = far[field].reshape(side, DEPTH)
        from_near = near[field].reshape(side, DEPTH)
        left = jnp.where(even, from_far, from_near) * has_left
        right = jnp.where(even, from_near, from_far) * has_right
        out = []
        for cells in ([left, rim[field, :64]], [rim[field, 64:], right]):
            parts = split(jnp.concatenate(cells, 0))
            out.append(jnp.concatenate(parts, 0))
        out = plane_blur(rim_matrix, jnp.concatenate(out, 1))
        out = jnp.where(is_right, out[:, DEPTH:], out[:, :DEPTH])
        edges.append(out)
        for row in range(ROWS):
            tail = jnp.concatenate(
                [last[field, row], out[row * 8 : (row + 1) * 8]], 0
            )
            tails[field * 4 + row // 2, row % 2] = jnp.concatenate(split(tail), 1)
    zero = jnp.zeros((64, DEPTH), F32)
    for first in range(0, 5, 2):
        parts = []
        for out in edges[first : first + 2]:
            parts += [out, zero]
        stack = jnp.concatenate(split(jnp.concatenate(parts, 0)), 1)
        out = depth_product(matrix[jnp.where(forward, 0, 1)], stack)
        for j in range(stack.shape[0] // 128):
            send[first + j] = out[:, j * 128 : (j + 1) * 128]
    for k in range(RADIUS):
        send[5 + k] = jnp.where(forward, class_t[DEPTH - RADIUS + k], class_t[k]).astype(F32)


def shade_cell(values, label, tables, scale, state):
    trans, s_sum, r_sum, g_sum, b_sum, step_sum = state
    linears = []
    for channel in range(4):
        entry = [
            jnp.take_along_axis(
                tables[channel * 6 + i], label, axis=0, mode="promise_in_bounds"
            )
            for i in range(6)
        ]
        linear = entry[0] * values[0] + entry[5]
        for i in range(1, 5):
            linear = linear + entry[i] * values[i]
        linears.append(linear)
    tints = [jnp.tanh(linear) for linear in linears[:3]]
    x = linears[3]
    t = jnp.exp(-jnp.abs(x))
    series = t * (1.0 - t * (1.0 / 2 - t * (1.0 / 3)))
    soft = jnp.maximum(x, 0.0) + jnp.where(t < 0.01, series, jnp.log(1.0 + t))
    step = soft * scale
    opacity = step * (
        1.0 - step * (1.0 / 2 - step * (1.0 / 6 - step * (1.0 / 24 - step * (1.0 / 120))))
    )
    shade = trans * opacity
    return (
        trans - shade,
        s_sum + shade,
        r_sum + shade * tints[0],
        g_sum + shade * tints[1],
        b_sum + shade * tints[2],
        step_sum + step,
    )


def fresh_state():
    zero = jnp.zeros((ROWS, COLS), F32)
    return (jnp.ones((ROWS, COLS), F32), zero, zero, zero, zero, zero)


def join(near, far):
    trans = near[0]
    sums = [near[i] + trans * far[i] for i in range(1, 5)]
    return (trans * far[0], *sums, near[5] + far[5])


def choose(flag, one, other):
    return tuple(jnp.where(flag, a, b) for a, b in zip(one, other))


def inner_kernel(scale, bodies, tails, class_t, tables, matrix, out, halo, end, smooth):
    forward = shades_forward(lax.axis_index("tile"))
    depths = len(INNER_TARGETS)
    flat = smooth.reshape(5, depths * ROWS, COLS)
    flat_halo = halo.reshape(5, 8 * ROWS, COLS)
    flat_end = end.reshape(5, RADIUS * ROWS, COLS)

    def blur(index, carry):
        field = index // 4
        pair = index % 4
        stack = jnp.concatenate(
            [bodies[index, 0], tails[index, 0], bodies[index, 1], tails[index, 1]], 0
        )
        product = depth_product(matrix[...], stack)
        front, back = product[:8], product[8 + depths :]
        keep = jnp.where(forward, front, back)
        last = jnp.where(forward, back[:4], front[4:])
        for j in range(2):
            row = pair * 2 + j
            lanes = slice(j * 128, (j + 1) * 128)
            flat[field, pl.ds(row, depths, stride=ROWS), :] = product[8 : 8 + depths, lanes]
            flat_halo[field, pl.ds(row, 8, stride=ROWS), :] = keep[:, lanes]
            flat_end[field, pl.ds(row, RADIUS, stride=ROWS), :] = last[:, lanes]
        return carry

    lax.fori_loop(0, 20, blur, 0, unroll=20)
    unroll = 24

    def body(index, state):
        for k in range(unroll):
            depth = index * unroll + k
            state = shade_cell(
                [smooth[f, depth] for f in range(5)],
                class_t[RADIUS + depth],
                tables,
                scale,
                state,
            )
        return state

    state = lax.fori_loop(0, depths // unroll, body, fresh_state())
    for i in range(6):
        out[i] = state[i]


def edge_kernel(
    scale, n_slab, halo, end_cells, class_t, tables, inner, place, given, given_rim,
    full, to_two, to_three, mine, total,
):
    slab = lax.axis_index("slab")
    forward = shades_forward(lax.axis_index("tile"))
    is_first, is_last = slab == 0, slab == n_slab - 1
    alone = jnp.where(forward, is_first, is_last)
    arrived = jnp.where(alone, 0.0, 1.0)
    step_one = jnp.where(jnp.logical_and(forward, is_first), 0.0, scale)
    step_two = jnp.where(jnp.logical_and(jnp.logical_not(forward), is_last), 0.0, scale)
    step_end = jnp.where(jnp.where(forward, is_last, is_first), scale, 0.0)

    shape = (8, ROWS, COLS)
    own_row = lax.broadcasted_iota(jnp.int32, shape, 2) // 8 == lax.broadcasted_iota(
        jnp.int32, shape, 1
    )
    for f in range(5):
        sums = jnp.broadcast_to(given_rim[f][:, None, :], shape)
        sums = jnp.where(own_row, sums, 0.0).reshape(8 * ROWS, COLS)
        moved = jnp.dot(
            jnp.concatenate(split(sums), 1), place[...], preferred_element_type=F32
        ).reshape(shape)
        total[f] = halo[f] + (given[pl.ds(f * 8, 8)] + moved) * arrived

    one = two = end = fresh_state()
    for k in range(RADIUS):
        theirs = given_rim[5 + k].astype(jnp.int32)
        front, back = class_t[k], class_t[DEPTH - RADIUS + k]
        values = [total[f, k] for f in range(5)]
        one = shade_cell(values, jnp.where(forward, theirs, back), tables, step_one, one)
        values = [total[f, RADIUS + k] for f in range(5)]
        two = shade_cell(values, jnp.where(forward, front, theirs), tables, step_two, two)
        values = [end_cells[f, k] for f in range(5)]
        end = shade_cell(values, jnp.where(forward, back, front), tables, step_end, end)
    middle = tuple(inner[i] for i in range(6))

    before = join(end, middle)
    backward_part = join(before, one)
    backward_full = join(backward_part, two)
    forward_full = join(join(join(one, two), middle), end)
    all_of_it = choose(forward, forward_full, backward_full)

    def store(ref, state):
        for i in range(3):
            ref[i] = pltpu.roll(0.5 * (state[1] + state[2 + i]), RADIUS, 1)
        ref[3] = pltpu.roll(jnp.exp(-state[5]), RADIUS, 1)

    store(full, all_of_it)
    store(to_two, choose(jnp.logical_and(forward, slab % 2 == 1), one, all_of_it))
    store(to_three, choose(jnp.logical_and(forward, slab >= 2), one, all_of_it))
    store(mine, choose(forward, forward_full, backward_part))


def pair(ref):
    return [ref[i] for i in range(4)]


def over(near, far):
    return [near[i] + near[3] * far[i] for i in range(3)] + [near[3] * far[3]]


def only(flag, value):
    return [jnp.where(flag, value[i], 0.0) for i in range(3)] + [jnp.where(flag, value[3], 1.0)]


def final_kernel(got_one, got_two, got_three, mine, out):
    slab = lax.axis_index("slab")
    forward = shades_forward(lax.axis_index("tile"))
    by_one, by_two, by_three = pair(got_one), pair(got_two), pair(got_three)
    total = only(slab == 3, by_one)
    total = over(total, only(slab >= 2, by_three))
    total = over(total, only(jnp.logical_and(forward, slab == 2), by_one))
    total = over(total, only(jnp.where(forward, slab % 2 == 1, slab >= 1), by_two))
    total = over(total, pair(mine))
    total = over(total, only(jnp.logical_and(forward, slab % 2 == 0), by_two))
    total = over(total, only(jnp.logical_and(forward, slab == 1), by_three))
    for i in range(3):
        out[0, i] = total[i]
    out[0, 3] = 1.0 - total[3]


def in_vmem(*arrays):
    return tuple(pltpu.with_memory_space_constraint(a, VMEM) for a in arrays)


def in_hbm(*arrays):
    return tuple(pltpu.with_memory_space_constraint(a, pltpu.HBM) for a in arrays)


SPEC = pl.BlockSpec(memory_space=VMEM)
HBM_SPEC = pl.BlockSpec(memory_space=pltpu.HBM)
PARAMS = pltpu.CompilerParams(vmem_limit_bytes=32 * 1024 * 1024)


def cost(microseconds):
    return pl.CostEstimate(
        flops=int(microseconds * 1e9), bytes_accessed=int(microseconds * 3.6e6), transcendentals=0
    )


def permute(value, target):
    n_tile, n_slab = lax.axis_size("tile"), lax.axis_size("slab")
    pairs = []
    for t in range(n_tile):
        for s in range(n_slab):
            to_tile, to_slab = target(t, s)
            pairs.append((t * n_slab + s, to_tile * n_slab + to_slab))
    return lax.ppermute(value, ("tile", "slab"), pairs)


def on_device(counts, fields, class_ids, tf_table):
    n_tile, n_slab = lax.axis_size("tile"), lax.axis_size("slab")
    scale = OPTICAL / (DEPTH * n_slab)

    far, near = pl.pallas_call(
        pack_kernel,
        out_shape=[VMEM((5, RADIUS, ROWS, DEPTH), F32)] * 2,
        in_specs=[HBM_SPEC] * 2,
        out_specs=[SPEC] * 2,
        scratch_shapes=[VMEM((2, RADIUS, ROWS, DEPTH), jnp.int32), pltpu.SemaphoreType.DMA((4,))],
        compiler_params=PARAMS,
        cost_estimate=cost(1),
        name="pack",
    )(*in_hbm(counts, fields))

    def across(t, s):
        other = ((t + 1) ^ 1) - 1
        return (other, s) if 0 <= other < n_tile else (t, s ^ 1)

    far = permute(far, across)
    near = lax.ppermute(near, "tile", [(t, t ^ 1) for t in range(n_tile)])

    step_matrix = plane_matrix(list(range(RADIUS, RADIUS + WIDE)), list(range(2 * WIDE)))
    end_matrix = jnp.asarray(np.stack([depth_matrix(BACK_TARGETS), depth_matrix(FRONT_TARGETS)]))
    bodies, last, rim, send = pl.pallas_call(
        columns_kernel,
        out_shape=[
            VMEM((20, 2, BODY, 2 * DEPTH), BF16),
            VMEM((5, ROWS, WIDE, DEPTH), F32),
            VMEM((5, 16 * ROWS, DEPTH), F32),
            VMEM((40, ROWS, COLS), F32),
        ],
        in_specs=[SPEC] * 4,
        out_specs=[SPEC] * 4,
        scratch_shapes=[
            VMEM((5, COLS * ROWS, DEPTH), BF16),
            VMEM((5, COLS * ROWS, DEPTH), BF16),
        ],
        compiler_params=PARAMS,
        cost_estimate=cost(3),
        name="columns",
    )(*in_vmem(jnp.asarray(step_matrix), end_matrix, counts, fields))

    def beside(t, s):
        to = s + 1 if shades_forward(t) else s - 1
        return (t, to) if 0 <= to < n_slab else (t ^ 1, s)

    given = permute(send, beside)

    rim_matrix = plane_matrix(2 * list(range(RADIUS, 2 * RADIUS)), list(range(3 * RADIUS)))
    class_t, tables, tails, send_rim = pl.pallas_call(
        functools.partial(rim_kernel, n_tile),
        out_shape=[
            VMEM((DEPTH, ROWS, COLS), jnp.int32),
            VMEM((24, ROWS, 128), F32),
            VMEM((20, 2, COLS - BODY, 2 * DEPTH), BF16),
            VMEM((9, 8, 128), F32),
        ],
        in_specs=[SPEC] * 8,
        out_specs=[SPEC] * 4,
        compiler_params=PARAMS,
        cost_estimate=cost(1),
        name="rim",
    )(
        *in_vmem(
            jnp.transpose(tf_table, (2, 1, 0)), class_ids, last, rim, far, near,
            jnp.asarray(rim_matrix), end_matrix,
        )
    )
    given_rim = permute(send_rim, beside)

    depths = len(INNER_TARGETS)
    inner, halo, end_cells = pl.pallas_call(
        functools.partial(inner_kernel, scale),
        out_shape=[
            VMEM((6, ROWS, COLS), F32),
            VMEM((5, 8, ROWS, COLS), F32),
            VMEM((5, RADIUS, ROWS, COLS), F32),
        ],
        in_specs=[SPEC] * 5,
        out_specs=[SPEC] * 3,
        scratch_shapes=[VMEM((5, depths, ROWS, COLS), F32)],
        compiler_params=PARAMS,
        cost_estimate=cost(3.5),
        name="inner",
    )(
        *in_vmem(
            bodies, tails, class_t, tables,
            jnp.asarray(depth_matrix(FRONT_TARGETS + INNER_TARGETS + BACK_TARGETS)),
        )
    )

    place = np.zeros((2, COLS, COLS), np.float32)
    for lane in range(64):
        place[:, lane, INNER + lane % 8] = 1.0
    full, to_two, to_three, mine = pl.pallas_call(
        functools.partial(edge_kernel, scale, n_slab),
        out_shape=[VMEM((4, ROWS, COLS), F32)] * 4,
        in_specs=[SPEC] * 8,
        out_specs=[SPEC] * 4,
        scratch_shapes=[VMEM((5, 8, ROWS, COLS), F32)],
        compiler_params=PARAMS,
        cost_estimate=cost(0.5),
        name="edges",
    )(
        *in_vmem(
            halo, end_cells, class_t, tables, inner,
            jnp.asarray(place.reshape(2 * COLS, COLS), BF16), given, given_rim,
        )
    )

    def first(t, s):
        if shades_forward(t):
            return ((t, 3), (t, 2), (t ^ 1, 2), (t, 0))[s]
        return ((t, 3), (t ^ 1, 1), (t, 1), (t, 0))[s]

    def second(t, s):
        return (t, s ^ 1 if shades_forward(t) else (s + 1) % n_slab)

    got_one = permute(full, first)
    got_two = permute(to_two, second)
    got_three = permute(to_three, lambda t, s: (t, (2, 3, 1, 0)[s]))
    return pl.pallas_call(
        final_kernel,
        out_shape=jax.ShapeDtypeStruct((1, 4, ROWS, COLS), F32),
        in_specs=[SPEC] * 4,
        out_specs=SPEC,
        compiler_params=PARAMS,
        name="final",
    )(*in_vmem(got_one, got_two, got_three, mine))


def solution(mesh):
    return jax.shard_map(
        on_device,
        mesh=mesh,
        in_specs=(
            P("tile", None, "slab"),
            P(None, "tile", None, "slab"),
            P("tile", None, "slab"),
            P(),
        ),
        out_specs=P("slab", None, None, "tile"),
        check_vma=False,
    )
```

```python
import functools
import math

import jax
import jax.numpy as jnp
import numpy as np
from jax import lax
from jax.experimental import pallas as pl
from jax.experimental.pallas import tpu as pltpu
from jax.sharding import PartitionSpec as P

CLASSES = 8
RADIUS = 4
SPLAT = 2.0
OPTICAL = 0.5
COLS, ROWS, DEPTH = 128, 8, 128
F32, BF16 = jnp.float32, jnp.bfloat16
VMEM = pltpu.VMEM


def splat_taps():
    raw = [
        math.exp(-((offset - RADIUS) ** 2) / (2.0 * SPLAT * SPLAT))
        for offset in range(2 * RADIUS + 1)
    ]
    norm_total = sum(raw)
    return [value / norm_total for value in raw]


W = splat_taps()


def shades_forward(tile):
    return tile % 2 == 1


def tap(offset):
    return W[offset + RADIUS] if abs(offset) <= RADIUS else 0.0


def split_const(full):
    high = full.astype(jnp.bfloat16)
    return high, (full - high.astype(np.float64)).astype(jnp.bfloat16)


def split_rows(full):
    high, low = split_const(full)
    top = np.concatenate([high, high], 1)
    bottom = np.concatenate([low, np.zeros_like(low)], 1)
    return np.concatenate([top, bottom], 0)


def depth_matrix(targets):
    return split_rows(
        np.array([[tap(cell - target) for cell in range(DEPTH)] for target in targets])
    )


def plane_matrix(targets, cells):
    full = np.zeros((ROWS, len(targets), len(cells), ROWS), np.float64)
    for to_row in range(ROWS):
        for i, target in enumerate(targets):
            for j, cell in enumerate(cells):
                for row in range(ROWS):
                    full[to_row, i, j, row] = tap(cell - target) * tap(row - to_row)
    return split_rows(full.reshape(ROWS * len(targets), len(cells) * ROWS))


WIDE = 8
INNER = COLS - 2 * RADIUS
FRONT_TARGETS = list(range(-RADIUS, RADIUS))
INNER_TARGETS = list(range(RADIUS, DEPTH - RADIUS))
BACK_TARGETS = list(range(DEPTH - RADIUS, DEPTH + RADIUS))
BODY = 112


def split(value):
    high = value.astype(BF16)
    return high, (value - high.astype(F32)).astype(BF16)


def plane_blur(matrix, stack):
    out = jnp.dot(matrix[...], stack, preferred_element_type=F32)
    rows = matrix.shape[0] // 2
    return out[:rows] + out[rows:]


def pack_kernel(counts, fields, far, near, count_rows, sems):
    even = lax.axis_index("tile") % 2 == 0
    copies = []
    for i, (ref, at_start) in enumerate(((far, even), (near, jnp.logical_not(even)))):
        cells = pl.ds(jnp.where(at_start, 0, COLS - RADIUS), RADIUS)
        copies.append(pltpu.make_async_copy(counts.at[cells], count_rows.at[i], sems.at[2 * i]))
        copies.append(
            pltpu.make_async_copy(fields.at[:, cells], ref.at[pl.ds(1, 4)], sems.at[2 * i + 1])
        )
    for copy in copies:
        copy.start()
    for copy in copies:
        copy.wait()
    far[0] = jnp.log(1.0 + count_rows[0].astype(F32))
    near[0] = jnp.log(1.0 + count_rows[1].astype(F32))


def columns_kernel(
    matrix, end_matrix, table, class_v, count_v, field_v,
    bodies, last, rim, class_t, tables, send,
    high, low,
):
    lane = lax.broadcasted_iota(jnp.int32, (CLASSES, CLASSES), 1)
    row_index = lax.broadcasted_iota(jnp.int32, (CLASSES, CLASSES), 0)
    for channel in range(4):
        scale = 0.5 if channel < 3 else 1.0
        for coefficient in range(6):
            per_class = jnp.broadcast_to(
                table[coefficient, channel : channel + 1, :], (CLASSES, CLASSES)
            )
            column = jnp.sum(
                jnp.where(lane == row_index, per_class, 0.0), axis=1, keepdims=True
            )
            tables[channel * 6 + coefficient] = jnp.broadcast_to(column * scale, (CLASSES, 128))

    flat = class_v.reshape(COLS * ROWS, DEPTH)
    flat_t = class_t.reshape(DEPTH * ROWS, COLS)

    def turn(row):
        plane = flat[pl.ds(row, COLS, stride=ROWS), :]
        flat_t[pl.ds(row, DEPTH, stride=ROWS), :] = pltpu.roll(plane.T, COLS - RADIUS, 1)

    def prepare(source, field):
        rim[field, pl.ds(0, 64), :] = source[pl.ds(0, 64), :]
        rim[field, pl.ds(64, 64), :] = source[pl.ds((COLS - 8) * ROWS, 64), :]
        high[field], low[field] = split(source[...])

    def product(windows):
        sides = []
        for field, step in windows:
            cells = pl.ds(step * WIDE * ROWS, 2 * WIDE * ROWS)
            sides.append(jnp.concatenate([high[field, cells, :], low[field, cells, :]], 0))
        return plane_blur(matrix, jnp.concatenate(sides, 1))

    def sweep(field):
        for step in range(0, BODY // WIDE, 2):
            out = product([(field, step), (field, step + 1)])
            for row in range(ROWS):
                cut = out[row * WIDE : (row + 1) * WIDE]
                tile = jnp.concatenate([cut[:, :DEPTH], cut[:, DEPTH:]], 0)
                bodies[field * 4 + row // 2, row % 2, pl.ds(step * WIDE, 16)] = jnp.concatenate(
                    split(tile), 1
                )

    prepare(jnp.log(1.0 + count_v[...].astype(F32)).reshape(COLS * ROWS, DEPTH), 0)
    prepare(field_v.at[0].reshape(COLS * ROWS, DEPTH), 1)
    sweep(0)
    sweep(1)
    for field in range(1, 4):
        prepare(field_v.at[field].reshape(COLS * ROWS, DEPTH), field + 1)
    for field in range(2, 5):
        sweep(field)
        for row in range((field - 2) * 3, min((field - 1) * 3, ROWS)):
            turn(row)
    for first in range(0, 5, 2):
        windows = [(field, BODY // WIDE) for field in range(first, min(first + 2, 5))]
        out = product(windows)
        for j, (field, _) in enumerate(windows):
            last[field] = out[:, j * DEPTH : (j + 1) * DEPTH].reshape(ROWS, WIDE, DEPTH)

    forward = shades_forward(lax.axis_index("tile"))
    for k in range(RADIUS):
        send[40 + k] = jnp.where(forward, class_t[DEPTH - RADIUS + k], class_t[k]).astype(F32)
    flat_send = send.reshape(44 * ROWS, COLS)
    own_matrix = end_matrix[jnp.where(forward, 0, 1)]
    zero = jnp.zeros((8, DEPTH), F32)
    for index in range(20):
        field, pair = index // 4, index % 4
        parts = []
        for j in range(2):
            tail = jnp.concatenate([last[field, pair * 2 + j], zero], 0)
            parts += [bodies[index, j], jnp.concatenate(split(tail), 1)]
        out = depth_product(own_matrix, jnp.concatenate(parts, 0))
        for j in range(2):
            flat_send[pl.ds(field * 64 + pair * 2 + j, 8, stride=ROWS), :] = out[
                :, j * 128 : (j + 1) * 128
            ]


def depth_product(matrix, stack):
    out = lax.dot_general(
        matrix, stack, (((1,), (1,)), ((), ())), preferred_element_type=F32
    )
    half = matrix.shape[0] // 2
    return out[:half] + out[half:]


def rim_kernel(
    n_tile, last, rim, far, near, rim_matrix, matrix, tails, send
):
    tile = lax.axis_index("tile")
    even = tile % 2 == 0
    forward = shades_forward(tile)
    has_left = (tile > 0).astype(F32)
    has_right = (tile < n_tile - 1).astype(F32)
    side = RADIUS * ROWS
    is_right = lax.broadcasted_iota(jnp.int32, (8 * ROWS, DEPTH), 0) % 8 < RADIUS
    edges = []
    for field in range(5):
        from_far = far[field].reshape(side, DEPTH)
        from_near = near[field].reshape(side, DEPTH)
        left = jnp.where(even, from_far, from_near) * has_left
        right = jnp.where(even, from_near, from_far) * has_right
        out = []
        for cells in ([left, rim[field, :64]], [rim[field, 64:], right]):
            parts = split(jnp.concatenate(cells, 0))
            out.append(jnp.concatenate(parts, 0))
        out = plane_blur(rim_matrix, jnp.concatenate(out, 1))
        out = jnp.where(is_right, out[:, DEPTH:], out[:, :DEPTH])
        edges.append(out)
        for row in range(ROWS):
            tail = jnp.concatenate(
                [last[field, row], out[row * 8 : (row + 1) * 8]], 0
            )
            tails[field * 4 + row // 2, row % 2] = jnp.concatenate(split(tail), 1)
    zero = jnp.zeros((64, DEPTH), F32)
    for first in range(0, 5, 2):
        parts = []
        for out in edges[first : first + 2]:
            parts += [out, zero]
        stack = jnp.concatenate(split(jnp.concatenate(parts, 0)), 1)
        out = depth_product(matrix[jnp.where(forward, 0, 1)], stack)
        for j in range(stack.shape[0] // 128):
            send[first + j] = out[:, j * 128 : (j + 1) * 128]


def shade_cell(values, label, tables, scale, state):
    trans, s_sum, r_sum, g_sum, b_sum, step_sum = state
    linears = []
    for channel in range(4):
        entry = [
            jnp.take_along_axis(
                tables[channel * 6 + i], label, axis=0, mode="promise_in_bounds"
            )
            for i in range(6)
        ]
        linear = entry[0] * values[0] + entry[5]
        for i in range(1, 5):
            linear = linear + entry[i] * values[i]
        linears.append(linear)
    tints = [jnp.tanh(linear) for linear in linears[:3]]
    x = linears[3]
    t = jnp.exp(-jnp.abs(x))
    series = t * (1.0 - t * (1.0 / 2 - t * (1.0 / 3)))
    soft = jnp.maximum(x, 0.0) + jnp.where(t < 0.01, series, jnp.log(1.0 + t))
    step = soft * scale
    opacity = step * (
        1.0 - step * (1.0 / 2 - step * (1.0 / 6 - step * (1.0 / 24 - step * (1.0 / 120))))
    )
    shade = trans * opacity
    return (
        trans - shade,
        s_sum + shade,
        r_sum + shade * tints[0],
        g_sum + shade * tints[1],
        b_sum + shade * tints[2],
        step_sum + step,
    )


def fresh_state():
    zero = jnp.zeros((ROWS, COLS), F32)
    return (jnp.ones((ROWS, COLS), F32), zero, zero, zero, zero, zero)


def join(near, far):
    trans = near[0]
    sums = [near[i] + trans * far[i] for i in range(1, 5)]
    return (trans * far[0], *sums, near[5] + far[5])


def choose(flag, one, other):
    return tuple(jnp.where(flag, a, b) for a, b in zip(one, other))


def inner_kernel(scale, bodies, tails, class_t, tables, matrix, out, halo, end, smooth):
    forward = shades_forward(lax.axis_index("tile"))
    depths = len(INNER_TARGETS)
    flat = smooth.reshape(5, depths * ROWS, COLS)
    flat_halo = halo.reshape(5, 8 * ROWS, COLS)
    flat_end = end.reshape(5, RADIUS * ROWS, COLS)

    def blur(index, carry):
        field = index // 4
        pair = index % 4
        stack = jnp.concatenate(
            [bodies[index, 0], tails[index, 0], bodies[index, 1], tails[index, 1]], 0
        )
        product = depth_product(matrix[...], stack)
        front, back = product[:8], product[8 + depths :]
        keep = jnp.where(forward, front, back)
        last = jnp.where(forward, back[:4], front[4:])
        for j in range(2):
            row = pair * 2 + j
            lanes = slice(j * 128, (j + 1) * 128)
            flat[field, pl.ds(row, depths, stride=ROWS), :] = product[8 : 8 + depths, lanes]
            flat_halo[field, pl.ds(row, 8, stride=ROWS), :] = keep[:, lanes]
            flat_end[field, pl.ds(row, RADIUS, stride=ROWS), :] = last[:, lanes]
        return carry

    lax.fori_loop(0, 20, blur, 0, unroll=20)
    unroll = 24

    def body(index, state):
        for k in range(unroll):
            depth = index * unroll + k
            state = shade_cell(
                [smooth[f, depth] for f in range(5)],
                class_t[RADIUS + depth],
                tables,
                scale,
                state,
            )
        return state

    state = lax.fori_loop(0, depths // unroll, body, fresh_state())
    for i in range(6):
        out[i] = state[i]


def edge_kernel(
    scale, n_slab, halo, end_cells, class_t, tables, inner, place, given, given_rim,
    full, to_two, to_three, mine, total,
):
    slab = lax.axis_index("slab")
    forward = shades_forward(lax.axis_index("tile"))
    is_first, is_last = slab == 0, slab == n_slab - 1
    alone = jnp.where(forward, is_first, is_last)
    arrived = jnp.where(alone, 0.0, 1.0)
    step_one = jnp.where(jnp.logical_and(forward, is_first), 0.0, scale)
    step_two = jnp.where(jnp.logical_and(jnp.logical_not(forward), is_last), 0.0, scale)
    step_end = jnp.where(jnp.where(forward, is_last, is_first), scale, 0.0)

    shape = (8, ROWS, COLS)
    own_row = lax.broadcasted_iota(jnp.int32, shape, 2) // 8 == lax.broadcasted_iota(
        jnp.int32, shape, 1
    )
    for f in range(5):
        sums = jnp.broadcast_to(given_rim[f][:, None, :], shape)
        sums = jnp.where(own_row, sums, 0.0).reshape(8 * ROWS, COLS)
        moved = jnp.dot(
            jnp.concatenate(split(sums), 1), place[...], preferred_element_type=F32
        ).reshape(shape)
        total[f] = halo[f] + (given[pl.ds(f * 8, 8)] + moved) * arrived

    one = two = end = fresh_state()
    for k in range(RADIUS):
        theirs = given[40 + k].astype(jnp.int32)
        front, back = class_t[k], class_t[DEPTH - RADIUS + k]
        values = [total[f, k] for f in range(5)]
        one = shade_cell(values, jnp.where(forward, theirs, back), tables, step_one, one)
        values = [total[f, RADIUS + k] for f in range(5)]
        two = shade_cell(values, jnp.where(forward, front, theirs), tables, step_two, two)
        values = [end_cells[f, k] for f in range(5)]
        end = shade_cell(values, jnp.where(forward, back, front), tables, step_end, end)
    middle = tuple(inner[i] for i in range(6))

    before = join(end, middle)
    backward_part = join(before, one)
    backward_full = join(backward_part, two)
    forward_full = join(join(join(one, two), middle), end)
    all_of_it = choose(forward, forward_full, backward_full)

    def store(ref, state):
        for i in range(3):
            ref[i] = pltpu.roll(0.5 * (state[1] + state[2 + i]), RADIUS, 1)
        ref[3] = pltpu.roll(jnp.exp(-state[5]), RADIUS, 1)

    store(full, all_of_it)
    store(to_two, choose(jnp.logical_and(forward, slab >= 2), one, all_of_it))
    store(to_three, choose(jnp.logical_and(forward, slab % 2 == 1), one, all_of_it))
    store(mine, choose(forward, forward_full, backward_part))


def pair(ref):
    return [ref[i] for i in range(4)]


def over(near, far):
    return [near[i] + near[3] * far[i] for i in range(3)] + [near[3] * far[3]]


def only(flag, value):
    return [jnp.where(flag, value[i], 0.0) for i in range(3)] + [jnp.where(flag, value[3], 1.0)]


def final_kernel(got_one, got_two, got_three, mine, out):
    slab = lax.axis_index("slab")
    forward = shades_forward(lax.axis_index("tile"))
    sets = pair(got_one), pair(got_two), pair(got_three)

    def either(if_forward, if_not):
        return [jnp.where(forward, a, b) for a, b in zip(sets[if_forward], sets[if_not])]

    by_three, by_two, by_one = either(1, 0), either(0, 2), either(2, 1)
    total = only(slab == 3, by_three)
    total = over(total, only(slab >= 2, by_two))
    total = over(total, only(jnp.logical_and(forward, slab == 2), by_three))
    total = over(total, only(jnp.where(forward, slab % 2 == 1, slab >= 1), by_one))
    total = over(total, pair(mine))
    total = over(total, only(jnp.logical_and(forward, slab % 2 == 0), by_one))
    total = over(total, only(jnp.logical_and(forward, slab == 1), by_three))
    for i in range(3):
        out[0, i] = total[i]
    out[0, 3] = 1.0 - total[3]


def in_vmem(*arrays):
    return tuple(pltpu.with_memory_space_constraint(a, VMEM) for a in arrays)


def in_hbm(*arrays):
    return tuple(pltpu.with_memory_space_constraint(a, pltpu.HBM) for a in arrays)


SPEC = pl.BlockSpec(memory_space=VMEM)
HBM_SPEC = pl.BlockSpec(memory_space=pltpu.HBM)
PARAMS = pltpu.CompilerParams(vmem_limit_bytes=32 * 1024 * 1024)


def cost(microseconds):
    return pl.CostEstimate(
        flops=int(microseconds * 1e9), bytes_accessed=int(microseconds * 3.6e6), transcendentals=0
    )


def permute(value, target):
    n_tile, n_slab = lax.axis_size("tile"), lax.axis_size("slab")
    pairs = []
    for t in range(n_tile):
        for s in range(n_slab):
            to_tile, to_slab = target(t, s)
            pairs.append((t * n_slab + s, to_tile * n_slab + to_slab))
    return lax.ppermute(value, ("tile", "slab"), pairs)


def on_device(counts, fields, class_ids, tf_table):
    n_tile, n_slab = lax.axis_size("tile"), lax.axis_size("slab")
    scale = OPTICAL / (DEPTH * n_slab)

    far, near = pl.pallas_call(
        pack_kernel,
        out_shape=[VMEM((5, RADIUS, ROWS, DEPTH), F32)] * 2,
        in_specs=[HBM_SPEC] * 2,
        out_specs=[SPEC] * 2,
        scratch_shapes=[VMEM((2, RADIUS, ROWS, DEPTH), jnp.int32), pltpu.SemaphoreType.DMA((4,))],
        compiler_params=PARAMS,
        cost_estimate=cost(1),
        name="pack",
    )(*in_hbm(counts, fields))

    def across(t, s):
        other = ((t + 1) ^ 1) - 1
        return (other, s) if 0 <= other < n_tile else (t, s ^ 1)

    far = permute(far, across)
    near = lax.ppermute(near, "tile", [(t, t ^ 1) for t in range(n_tile)])

    step_matrix = plane_matrix(list(range(RADIUS, RADIUS + WIDE)), list(range(2 * WIDE)))
    end_matrix = jnp.asarray(np.stack([depth_matrix(BACK_TARGETS), depth_matrix(FRONT_TARGETS)]))
    bodies, last, rim, class_t, tables, send = pl.pallas_call(
        columns_kernel,
        out_shape=[
            VMEM((20, 2, BODY, 2 * DEPTH), BF16),
            VMEM((5, ROWS, WIDE, DEPTH), F32),
            VMEM((5, 16 * ROWS, DEPTH), F32),
            VMEM((DEPTH, ROWS, COLS), jnp.int32),
            VMEM((24, ROWS, 128), F32),
            VMEM((44, ROWS, COLS), F32),
        ],
        in_specs=[SPEC] * 6,
        out_specs=[SPEC] * 6,
        scratch_shapes=[
            VMEM((5, COLS * ROWS, DEPTH), BF16),
            VMEM((5, COLS * ROWS, DEPTH), BF16),
        ],
        compiler_params=PARAMS,
        cost_estimate=cost(3),
        name="columns",
    )(
        *in_vmem(
            jnp.asarray(step_matrix), end_matrix, jnp.transpose(tf_table, (2, 1, 0)),
            class_ids, counts, fields,
        )
    )

    def beside(t, s):
        to = s + 1 if shades_forward(t) else s - 1
        return (t, to) if 0 <= to < n_slab else (t ^ 1, s)

    given = permute(send, beside)

    rim_matrix = plane_matrix(2 * list(range(RADIUS, 2 * RADIUS)), list(range(3 * RADIUS)))
    tails, send_rim = pl.pallas_call(
        functools.partial(rim_kernel, n_tile),
        out_shape=[VMEM((20, 2, COLS - BODY, 2 * DEPTH), BF16), VMEM((5, 8, 128), F32)],
        in_specs=[SPEC] * 6,
        out_specs=[SPEC] * 2,
        compiler_params=PARAMS,
        cost_estimate=cost(0.5),
        name="rim",
    )(*in_vmem(last, rim, far, near, jnp.asarray(rim_matrix), end_matrix))
    given_rim = permute(send_rim, beside)

    depths = len(INNER_TARGETS)
    inner, halo, end_cells = pl.pallas_call(
        functools.partial(inner_kernel, scale),
        out_shape=[
            VMEM((6, ROWS, COLS), F32),
            VMEM((5, 8, ROWS, COLS), F32),
            VMEM((5, RADIUS, ROWS, COLS), F32),
        ],
        in_specs=[SPEC] * 5,
        out_specs=[SPEC] * 3,
        scratch_shapes=[VMEM((5, depths, ROWS, COLS), F32)],
        compiler_params=PARAMS,
        cost_estimate=cost(3.5),
        name="inner",
    )(
        *in_vmem(
            bodies, tails, class_t, tables,
            jnp.asarray(depth_matrix(FRONT_TARGETS + INNER_TARGETS + BACK_TARGETS)),
        )
    )

    place = np.zeros((2, COLS, COLS), np.float32)
    for lane in range(64):
        place[:, lane, INNER + lane % 8] = 1.0
    full, to_two, to_three, mine = pl.pallas_call(
        functools.partial(edge_kernel, scale, n_slab),
        out_shape=[VMEM((4, ROWS, COLS), F32)] * 4,
        in_specs=[SPEC] * 8,
        out_specs=[SPEC] * 4,
        scratch_shapes=[VMEM((5, 8, ROWS, COLS), F32)],
        compiler_params=PARAMS,
        cost_estimate=cost(0.5),
        name="edges",
    )(
        *in_vmem(
            halo, end_cells, class_t, tables, inner,
            jnp.asarray(place.reshape(2 * COLS, COLS), BF16), given, given_rim,
        )
    )

    def first(t, s):
        if shades_forward(t):
            return ((t, 2), (t, 3), (t ^ 1, 2), (t, 0))[s]
        return ((t, 3), (t ^ 1, 1), (t, 1), (t, 0))[s]

    def second(t, s):
        return (t, s ^ 3 if shades_forward(t) else (s + 1) % n_slab)

    def third(t, s):
        return (t, s ^ 1 if shades_forward(t) else (2, 3, 1, 0)[s])

    got_one = permute(full, first)
    got_two = permute(to_two, second)
    got_three = permute(to_three, third)
    return pl.pallas_call(
        final_kernel,
        out_shape=jax.ShapeDtypeStruct((1, 4, ROWS, COLS), F32),
        in_specs=[SPEC] * 4,
        out_specs=SPEC,
        compiler_params=PARAMS,
        name="final",
    )(*in_vmem(got_one, got_two, got_three, mine))


def solution(mesh):
    return jax.shard_map(
        on_device,
        mesh=mesh,
        in_specs=(
            P("tile", None, "slab"),
            P(None, "tile", None, "slab"),
            P("tile", None, "slab"),
            P(),
        ),
        out_specs=P("slab", None, None, "tile"),
        check_vma=False,
    )
```

```python
import functools
import math

import jax
import jax.numpy as jnp
import numpy as np
from jax import lax
from jax.experimental import pallas as pl
from jax.experimental.pallas import tpu as pltpu
from jax.sharding import PartitionSpec as P

CLASSES = 8
RADIUS = 4
SPLAT = 2.0
OPTICAL = 0.5
COLS, ROWS, DEPTH = 128, 8, 128
F32, BF16 = jnp.float32, jnp.bfloat16
VMEM = pltpu.VMEM


def splat_taps():
    raw = [
        math.exp(-((offset - RADIUS) ** 2) / (2.0 * SPLAT * SPLAT))
        for offset in range(2 * RADIUS + 1)
    ]
    norm_total = sum(raw)
    return [value / norm_total for value in raw]


W = splat_taps()


def shades_forward(tile):
    return tile % 2 == 1


def tap(offset):
    return W[offset + RADIUS] if abs(offset) <= RADIUS else 0.0


def split_const(full):
    high = full.astype(jnp.bfloat16)
    return high, (full - high.astype(np.float64)).astype(jnp.bfloat16)


def split_rows(full):
    high, low = split_const(full)
    top = np.concatenate([high, high], 1)
    bottom = np.concatenate([low, np.zeros_like(low)], 1)
    return np.concatenate([top, bottom], 0)


def depth_matrix(targets):
    return split_rows(
        np.array([[tap(cell - target) for cell in range(DEPTH)] for target in targets])
    )


def plane_matrix(targets, cells):
    full = np.zeros((ROWS, len(targets), len(cells), ROWS), np.float64)
    for to_row in range(ROWS):
        for i, target in enumerate(targets):
            for j, cell in enumerate(cells):
                for row in range(ROWS):
                    full[to_row, i, j, row] = tap(cell - target) * tap(row - to_row)
    return split_rows(full.reshape(ROWS * len(targets), len(cells) * ROWS))


WIDE = 8
INNER = COLS - 2 * RADIUS
FRONT_TARGETS = list(range(-RADIUS, RADIUS))
INNER_TARGETS = list(range(RADIUS, DEPTH - RADIUS))
BACK_TARGETS = list(range(DEPTH - RADIUS, DEPTH + RADIUS))
BODY = 112


def split(value):
    high = value.astype(BF16)
    return high, (value - high.astype(F32)).astype(BF16)


def plane_blur(matrix, stack):
    out = jnp.dot(matrix[...], stack, preferred_element_type=F32)
    rows = matrix.shape[0] // 2
    return out[:rows] + out[rows:]


def pack_kernel(counts, fields, far, near, count_rows, sems):
    even = lax.axis_index("tile") % 2 == 0
    copies = []
    for i, (ref, at_start) in enumerate(((far, even), (near, jnp.logical_not(even)))):
        cells = pl.ds(jnp.where(at_start, 0, COLS - RADIUS), RADIUS)
        copies.append(pltpu.make_async_copy(counts.at[cells], count_rows.at[i], sems.at[2 * i]))
        copies.append(
            pltpu.make_async_copy(fields.at[:, cells], ref.at[pl.ds(1, 4)], sems.at[2 * i + 1])
        )
    for copy in copies:
        copy.start()
    for copy in copies:
        copy.wait()
    far[0] = jnp.log(1.0 + count_rows[0].astype(F32))
    near[0] = jnp.log(1.0 + count_rows[1].astype(F32))


def columns_kernel(
    matrix, end_matrix, table, class_v, count_v, field_v,
    bodies, last, rim, class_t, tables, send,
    high, low,
):
    lane = lax.broadcasted_iota(jnp.int32, (CLASSES, CLASSES), 1)
    row_index = lax.broadcasted_iota(jnp.int32, (CLASSES, CLASSES), 0)
    for channel in range(4):
        scale = 0.5 if channel < 3 else 1.0
        for coefficient in range(6):
            per_class = jnp.broadcast_to(
                table[coefficient, channel : channel + 1, :], (CLASSES, CLASSES)
            )
            column = jnp.sum(
                jnp.where(lane == row_index, per_class, 0.0), axis=1, keepdims=True
            )
            tables[channel * 6 + coefficient] = jnp.broadcast_to(column * scale, (CLASSES, 128))

    flat = class_v.reshape(COLS * ROWS, DEPTH)
    flat_t = class_t.reshape(DEPTH * ROWS, COLS)

    def turn(row):
        plane = flat[pl.ds(row, COLS, stride=ROWS), :]
        flat_t[pl.ds(row, DEPTH, stride=ROWS), :] = pltpu.roll(plane.T, COLS - RADIUS, 1)

    def prepare(source, field):
        rim[field, pl.ds(0, 64), :] = source[pl.ds(0, 64), :]
        rim[field, pl.ds(64, 64), :] = source[pl.ds((COLS - 8) * ROWS, 64), :]
        high[field], low[field] = split(source[...])

    def product(windows):
        sides = []
        for field, step in windows:
            cells = pl.ds(step * WIDE * ROWS, 2 * WIDE * ROWS)
            sides.append(jnp.concatenate([high[field, cells, :], low[field, cells, :]], 0))
        return plane_blur(matrix, jnp.concatenate(sides, 1))

    def sweep(field):
        for step in range(0, BODY // WIDE, 2):
            out = product([(field, step), (field, step + 1)])
            for row in range(ROWS):
                cut = out[row * WIDE : (row + 1) * WIDE]
                tile = jnp.concatenate([cut[:, :DEPTH], cut[:, DEPTH:]], 0)
                bodies[field * 4 + row // 2, row % 2, pl.ds(step * WIDE, 16)] = jnp.concatenate(
                    split(tile), 1
                )

    prepare(jnp.log(1.0 + count_v[...].astype(F32)).reshape(COLS * ROWS, DEPTH), 0)
    prepare(field_v.at[0].reshape(COLS * ROWS, DEPTH), 1)
    sweep(0)
    sweep(1)
    for field in range(1, 4):
        prepare(field_v.at[field].reshape(COLS * ROWS, DEPTH), field + 1)
    for field in range(2, 5):
        sweep(field)
        for row in range((field - 2) * 3, min((field - 1) * 3, ROWS)):
            turn(row)
    for first in range(0, 5, 2):
        windows = [(field, BODY // WIDE) for field in range(first, min(first + 2, 5))]
        out = product(windows)
        for j, (field, _) in enumerate(windows):
            last[field] = out[:, j * DEPTH : (j + 1) * DEPTH].reshape(ROWS, WIDE, DEPTH)

    forward = shades_forward(lax.axis_index("tile"))
    for k in range(RADIUS):
        send[40 + k] = jnp.where(forward, class_t[DEPTH - RADIUS + k], class_t[k]).astype(F32)
    flat_send = send.reshape(44 * ROWS, COLS)
    own_matrix = end_matrix[jnp.where(forward, 0, 1)]
    zero = jnp.zeros((8, DEPTH), F32)
    for index in range(20):
        field, pair = index // 4, index % 4
        parts = []
        for j in range(2):
            tail = jnp.concatenate([last[field, pair * 2 + j], zero], 0)
            parts += [bodies[index, j], jnp.concatenate(split(tail), 1)]
        out = depth_product(own_matrix, jnp.concatenate(parts, 0))
        for j in range(2):
            flat_send[pl.ds(field * 64 + pair * 2 + j, 8, stride=ROWS), :] = out[
                :, j * 128 : (j + 1) * 128
            ]


def depth_product(matrix, stack):
    out = lax.dot_general(
        matrix, stack, (((1,), (1,)), ((), ())), preferred_element_type=F32
    )
    half = matrix.shape[0] // 2
    return out[:half] + out[half:]


def rim_kernel(
    n_tile, last, rim, far, near, rim_matrix, matrix, tails, send
):
    tile = lax.axis_index("tile")
    even = tile % 2 == 0
    forward = shades_forward(tile)
    has_left = (tile > 0).astype(F32)
    has_right = (tile < n_tile - 1).astype(F32)
    side = RADIUS * ROWS
    is_right = lax.broadcasted_iota(jnp.int32, (8 * ROWS, DEPTH), 0) % 8 < RADIUS
    edges = []
    for field in range(5):
        from_far = far[field].reshape(side, DEPTH)
        from_near = near[field].reshape(side, DEPTH)
        left = jnp.where(even, from_far, from_near) * has_left
        right = jnp.where(even, from_near, from_far) * has_right
        out = []
        for cells in ([left, rim[field, :64]], [rim[field, 64:], right]):
            parts = split(jnp.concatenate(cells, 0))
            out.append(jnp.concatenate(parts, 0))
        out = plane_blur(rim_matrix, jnp.concatenate(out, 1))
        out = jnp.where(is_right, out[:, DEPTH:], out[:, :DEPTH])
        edges.append(out)
        for row in range(ROWS):
            tail = jnp.concatenate(
                [last[field, row], out[row * 8 : (row + 1) * 8]], 0
            )
            tails[field * 4 + row // 2, row % 2] = jnp.concatenate(split(tail), 1)
    zero = jnp.zeros((64, DEPTH), F32)
    for first in range(0, 5, 2):
        parts = []
        for out in edges[first : first + 2]:
            parts += [out, zero]
        stack = jnp.concatenate(split(jnp.concatenate(parts, 0)), 1)
        out = depth_product(matrix[jnp.where(forward, 0, 1)], stack)
        for j in range(stack.shape[0] // 128):
            send[first + j] = out[:, j * 128 : (j + 1) * 128]


def shade_cell(values, label, tables, scale, state):
    trans, s_sum, r_sum, g_sum, b_sum, step_sum = state
    linears = []
    for channel in range(4):
        entry = [
            jnp.take_along_axis(
                tables[channel * 6 + i], label, axis=0, mode="promise_in_bounds"
            )
            for i in range(6)
        ]
        linear = entry[0] * values[0] + entry[5]
        for i in range(1, 5):
            linear = linear + entry[i] * values[i]
        linears.append(linear)
    tints = [jnp.tanh(linear) for linear in linears[:3]]
    x = linears[3]
    t = jnp.exp(-jnp.abs(x))
    series = t * (1.0 - t * (1.0 / 2 - t * (1.0 / 3)))
    soft = jnp.maximum(x, 0.0) + jnp.where(t < 0.01, series, jnp.log(1.0 + t))
    step = soft * scale
    opacity = step * (
        1.0 - step * (1.0 / 2 - step * (1.0 / 6 - step * (1.0 / 24 - step * (1.0 / 120))))
    )
    shade = trans * opacity
    return (
        trans - shade,
        s_sum + shade,
        r_sum + shade * tints[0],
        g_sum + shade * tints[1],
        b_sum + shade * tints[2],
        step_sum + step,
    )


def fresh_state():
    zero = jnp.zeros((ROWS, COLS), F32)
    return (jnp.ones((ROWS, COLS), F32), zero, zero, zero, zero, zero)


def join(near, far):
    trans = near[0]
    sums = [near[i] + trans * far[i] for i in range(1, 5)]
    return (trans * far[0], *sums, near[5] + far[5])


def choose(flag, one, other):
    return tuple(jnp.where(flag, a, b) for a, b in zip(one, other))


def inner_kernel(scale, n_slab, bodies, tails, class_t, tables, matrix, out, halo, end, smooth):
    forward = shades_forward(lax.axis_index("tile"))
    depths = len(INNER_TARGETS)
    flat = smooth.reshape(5, depths * ROWS, COLS)
    flat_halo = halo.reshape(5, 8 * ROWS, COLS)
    flat_end = end.reshape(5, RADIUS * ROWS, COLS)

    def blur(index, carry):
        field = index // 4
        pair = index % 4
        stack = jnp.concatenate(
            [bodies[index, 0], tails[index, 0], bodies[index, 1], tails[index, 1]], 0
        )
        product = depth_product(matrix[...], stack)
        front, back = product[:8], product[8 + depths :]
        keep = jnp.where(forward, front, back)
        last = jnp.where(forward, back[:4], front[4:])
        for j in range(2):
            row = pair * 2 + j
            lanes = slice(j * 128, (j + 1) * 128)
            flat[field, pl.ds(row, depths, stride=ROWS), :] = product[8 : 8 + depths, lanes]
            flat_halo[field, pl.ds(row, 8, stride=ROWS), :] = keep[:, lanes]
            flat_end[field, pl.ds(row, RADIUS, stride=ROWS), :] = last[:, lanes]
        return carry

    lax.fori_loop(0, 20, blur, 0, unroll=20)
    unroll = 24

    def body(index, state):
        for k in range(unroll):
            depth = index * unroll + k
            state = shade_cell(
                [smooth[f, depth] for f in range(5)],
                class_t[RADIUS + depth],
                tables,
                scale,
                state,
            )
        return state

    state = lax.fori_loop(0, depths // unroll, body, fresh_state())
    slab = lax.axis_index("slab")
    shades_end = jnp.where(forward, slab == n_slab - 1, slab == 0)
    step_end = jnp.where(shades_end, scale, 0.0)
    last_state = fresh_state()
    for k in range(RADIUS):
        label = jnp.where(forward, class_t[DEPTH - RADIUS + k], class_t[k])
        values = [end[f, k] for f in range(5)]
        last_state = shade_cell(values, label, tables, step_end, last_state)
    for i in range(6):
        out[i] = state[i]
        out[6 + i] = last_state[i]


def edge_kernel(
    scale, n_slab, halo, class_t, tables, inner, place, given, given_rim,
    full, to_two, to_three, mine, total,
):
    slab = lax.axis_index("slab")
    forward = shades_forward(lax.axis_index("tile"))
    is_first, is_last = slab == 0, slab == n_slab - 1
    alone = jnp.where(forward, is_first, is_last)
    arrived = jnp.where(alone, 0.0, 1.0)
    step_one = jnp.where(jnp.logical_and(forward, is_first), 0.0, scale)
    step_two = jnp.where(jnp.logical_and(jnp.logical_not(forward), is_last), 0.0, scale)

    shape = (8, ROWS, COLS)
    own_row = lax.broadcasted_iota(jnp.int32, shape, 2) // 8 == lax.broadcasted_iota(
        jnp.int32, shape, 1
    )
    for f in range(5):
        sums = jnp.broadcast_to(given_rim[f][:, None, :], shape)
        sums = jnp.where(own_row, sums, 0.0).reshape(8 * ROWS, COLS)
        moved = jnp.dot(
            jnp.concatenate(split(sums), 1), place[...], preferred_element_type=F32
        ).reshape(shape)
        total[f] = halo[f] + (given[pl.ds(f * 8, 8)] + moved) * arrived

    one = two = fresh_state()
    for k in range(RADIUS):
        theirs = given[40 + k].astype(jnp.int32)
        front, back = class_t[k], class_t[DEPTH - RADIUS + k]
        values = [total[f, k] for f in range(5)]
        one = shade_cell(values, jnp.where(forward, theirs, back), tables, step_one, one)
        values = [total[f, RADIUS + k] for f in range(5)]
        two = shade_cell(values, jnp.where(forward, front, theirs), tables, step_two, two)
    middle = tuple(inner[i] for i in range(6))
    end = tuple(inner[6 + i] for i in range(6))

    before = join(end, middle)
    backward_part = join(before, one)
    backward_full = join(backward_part, two)
    forward_full = join(join(join(one, two), middle), end)
    all_of_it = choose(forward, forward_full, backward_full)

    def store(ref, state):
        for i in range(3):
            ref[i] = pltpu.roll(0.5 * (state[1] + state[2 + i]), RADIUS, 1)
        ref[3] = pltpu.roll(jnp.exp(-state[5]), RADIUS, 1)

    store(full, all_of_it)
    store(to_two, choose(jnp.logical_and(forward, slab >= 2), one, all_of_it))
    store(to_three, choose(jnp.logical_and(forward, slab % 2 == 1), one, all_of_it))
    store(mine, choose(forward, forward_full, backward_part))


def pair(ref):
    return [ref[i] for i in range(4)]


def over(near, far):
    return [near[i] + near[3] * far[i] for i in range(3)] + [near[3] * far[3]]


def only(flag, value):
    return [jnp.where(flag, value[i], 0.0) for i in range(3)] + [jnp.where(flag, value[3], 1.0)]


def final_kernel(got_one, got_two, got_three, mine, out):
    slab = lax.axis_index("slab")
    forward = shades_forward(lax.axis_index("tile"))
    sets = pair(got_one), pair(got_two), pair(got_three)

    def either(if_forward, if_not):
        return [jnp.where(forward, a, b) for a, b in zip(sets[if_forward], sets[if_not])]

    by_three, by_two, by_one = either(1, 0), either(0, 2), either(2, 1)
    total = only(slab == 3, by_three)
    total = over(total, only(slab >= 2, by_two))
    total = over(total, only(jnp.logical_and(forward, slab == 2), by_three))
    total = over(total, only(jnp.where(forward, slab % 2 == 1, slab >= 1), by_one))
    total = over(total, pair(mine))
    total = over(total, only(jnp.logical_and(forward, slab % 2 == 0), by_one))
    total = over(total, only(jnp.logical_and(forward, slab == 1), by_three))
    for i in range(3):
        out[0, i] = total[i]
    out[0, 3] = 1.0 - total[3]


def in_vmem(*arrays):
    return tuple(pltpu.with_memory_space_constraint(a, VMEM) for a in arrays)


def in_hbm(*arrays):
    return tuple(pltpu.with_memory_space_constraint(a, pltpu.HBM) for a in arrays)


SPEC = pl.BlockSpec(memory_space=VMEM)
HBM_SPEC = pl.BlockSpec(memory_space=pltpu.HBM)
PARAMS = pltpu.CompilerParams(vmem_limit_bytes=32 * 1024 * 1024)


def cost(microseconds):
    return pl.CostEstimate(
        flops=int(microseconds * 1e9), bytes_accessed=int(microseconds * 3.6e6), transcendentals=0
    )


def permute(value, target):
    n_tile, n_slab = lax.axis_size("tile"), lax.axis_size("slab")
    pairs = []
    for t in range(n_tile):
        for s in range(n_slab):
            to_tile, to_slab = target(t, s)
            pairs.append((t * n_slab + s, to_tile * n_slab + to_slab))
    return lax.ppermute(value, ("tile", "slab"), pairs)


def on_device(counts, fields, class_ids, tf_table):
    n_tile, n_slab = lax.axis_size("tile"), lax.axis_size("slab")
    scale = OPTICAL / (DEPTH * n_slab)

    far, near = pl.pallas_call(
        pack_kernel,
        out_shape=[VMEM((5, RADIUS, ROWS, DEPTH), F32)] * 2,
        in_specs=[HBM_SPEC] * 2,
        out_specs=[SPEC] * 2,
        scratch_shapes=[VMEM((2, RADIUS, ROWS, DEPTH), jnp.int32), pltpu.SemaphoreType.DMA((4,))],
        compiler_params=PARAMS,
        cost_estimate=cost(1),
        name="pack",
    )(*in_hbm(counts, fields))

    def across(t, s):
        other = ((t + 1) ^ 1) - 1
        return (other, s) if 0 <= other < n_tile else (t, s ^ 1)

    far = permute(far, across)
    near = lax.ppermute(near, "tile", [(t, t ^ 1) for t in range(n_tile)])

    step_matrix = plane_matrix(list(range(RADIUS, RADIUS + WIDE)), list(range(2 * WIDE)))
    end_matrix = jnp.asarray(np.stack([depth_matrix(BACK_TARGETS), depth_matrix(FRONT_TARGETS)]))
    bodies, last, rim, class_t, tables, send = pl.pallas_call(
        columns_kernel,
        out_shape=[
            VMEM((20, 2, BODY, 2 * DEPTH), BF16),
            VMEM((5, ROWS, WIDE, DEPTH), F32),
            VMEM((5, 16 * ROWS, DEPTH), F32),
            VMEM((DEPTH, ROWS, COLS), jnp.int32),
            VMEM((24, ROWS, 128), F32),
            VMEM((44, ROWS, COLS), F32),
        ],
        in_specs=[SPEC] * 6,
        out_specs=[SPEC] * 6,
        scratch_shapes=[
            VMEM((5, COLS * ROWS, DEPTH), BF16),
            VMEM((5, COLS * ROWS, DEPTH), BF16),
        ],
        compiler_params=PARAMS,
        cost_estimate=cost(3),
        name="columns",
    )(
        *in_vmem(
            jnp.asarray(step_matrix), end_matrix, jnp.transpose(tf_table, (2, 1, 0)),
            class_ids, counts, fields,
        )
    )

    def beside(t, s):
        to = s + 1 if shades_forward(t) else s - 1
        return (t, to) if 0 <= to < n_slab else (t ^ 1, s)

    given = permute(send, beside)

    rim_matrix = plane_matrix(2 * list(range(RADIUS, 2 * RADIUS)), list(range(3 * RADIUS)))
    tails, send_rim = pl.pallas_call(
        functools.partial(rim_kernel, n_tile),
        out_shape=[VMEM((20, 2, COLS - BODY, 2 * DEPTH), BF16), VMEM((5, 8, 128), F32)],
        in_specs=[SPEC] * 6,
        out_specs=[SPEC] * 2,
        compiler_params=PARAMS,
        cost_estimate=cost(0.5),
        name="rim",
    )(*in_vmem(last, rim, far, near, jnp.asarray(rim_matrix), end_matrix))
    given_rim = permute(send_rim, beside)

    depths = len(INNER_TARGETS)
    inner, halo = pl.pallas_call(
        functools.partial(inner_kernel, scale, n_slab),
        out_shape=[
            VMEM((12, ROWS, COLS), F32),
            VMEM((5, 8, ROWS, COLS), F32),
        ],
        in_specs=[SPEC] * 5,
        out_specs=[SPEC] * 2,
        scratch_shapes=[
            VMEM((5, RADIUS, ROWS, COLS), F32),
            VMEM((5, depths, ROWS, COLS), F32),
        ],
        compiler_params=PARAMS,
        cost_estimate=cost(3.5),
        name="inner",
    )(
        *in_vmem(
            bodies, tails, class_t, tables,
            jnp.asarray(depth_matrix(FRONT_TARGETS + INNER_TARGETS + BACK_TARGETS)),
        )
    )

    place = np.zeros((2, COLS, COLS), np.float32)
    for lane in range(64):
        place[:, lane, INNER + lane % 8] = 1.0
    full, to_two, to_three, mine = pl.pallas_call(
        functools.partial(edge_kernel, scale, n_slab),
        out_shape=[VMEM((4, ROWS, COLS), F32)] * 4,
        in_specs=[SPEC] * 7,
        out_specs=[SPEC] * 4,
        scratch_shapes=[VMEM((5, 8, ROWS, COLS), F32)],
        compiler_params=PARAMS,
        cost_estimate=cost(0.5),
        name="edges",
    )(
        *in_vmem(
            halo, class_t, tables, inner,
            jnp.asarray(place.reshape(2 * COLS, COLS), BF16), given, given_rim,
        )
    )

    def first(t, s):
        if shades_forward(t):
            return ((t, 2), (t, 3), (t ^ 1, 2), (t, 0))[s]
        return ((t, 3), (t ^ 1, 1), (t, 1), (t, 0))[s]

    def second(t, s):
        return (t, s ^ 3 if shades_forward(t) else (s + 1) % n_slab)

    def third(t, s):
        return (t, s ^ 1 if shades_forward(t) else (2, 3, 1, 0)[s])

    got_one = permute(full, first)
    got_two = permute(to_two, second)
    got_three = permute(to_three, third)
    return pl.pallas_call(
        final_kernel,
        out_shape=jax.ShapeDtypeStruct((1, 4, ROWS, COLS), F32),
        in_specs=[SPEC] * 4,
        out_specs=SPEC,
        compiler_params=PARAMS,
        name="final",
    )(*in_vmem(got_one, got_two, got_three, mine))


def solution(mesh):
    return jax.shard_map(
        on_device,
        mesh=mesh,
        in_specs=(
            P("tile", None, "slab"),
            P(None, "tile", None, "slab"),
            P("tile", None, "slab"),
            P(),
        ),
        out_specs=P("slab", None, None, "tile"),
        check_vma=False,
    )
```
